32 devices in a mesh: group: 16 (over z, y, core), inner: 2 (over x).
Axes of the slice: x: 2, y: 2, z: 4, core: 2. Of those that a mesh axis runs over, the one named last changes fastest.
Arguments:
- features: bfloat16 [49152, 768], P(('group', 'inner')), may hold values from -6 to 6
- projection: bfloat16 [768, 256], replicated, may hold values from -0.21875 to 0.21875
- adjacency: bfloat16 [49152, 512], P(('group', 'inner'))
- degree: int32 [49152], P(('group', 'inner')), may hold values from 2 to 9
- tile_src: int32 [384, 4], P(('group', 'inner')), may hold values from 0 to 31, as said below
- send_ids: int32 [32, 2, 2], P(('group', 'inner')), may hold values from 0 to 11, as said below
- send_count: int32 [32, 2], P(('group', 'inner')), may hold values from 1 to 2
- edge_ids: int32 [32, 2, 8], P(('group', 'inner')), may hold values from 0 to 11, as said below
- edge_count: int32 [32, 2], P(('group', 'inner')), may hold values from 1 to 8
- train_ids: int32 [32, 2, 64], P(('group', 'inner')), may hold values from 0 to 1535
Outputs:
- train_rows: bfloat16 [4096, 512], P(('group', 'inner'))
The draws below stay inside these ranges and needn't reach their ends.
Inputs may be any that keep to these rules, and one draw needn't show every extreme that they name: `tile_src`: codes name only live sources: an own block, a live slot of another partition of the same group (never the own inner index), or a live slot of a neighbouring group's partition. `send_ids`: the 2 ids of one list are distinct. `edge_ids`: the 8 ids of one list are distinct.
All inputs are finite; a program needn't handle non-finite values.
Results may differ from the reference program's by a relative error of at most 0.0054.
Values may be sent and summed in bfloat16 or wider, within the bound.
No kernel may reach another device: no remote copies, remote signals or barrier semaphores. Data moves between devices by JAX's collectives and lax.ppermute only.
A program may use at most 64 MiB of HBM per device.

```python
import jax
import jax.numpy as jnp
from jax import lax

F = 768
K = 256
TILE = 128
BLK = 12
TPB = 4
CAP = 2
CAPG = 8
TSLOT = 64
GROUPS = 16
OWNERS = 2
PARTITIONS = 32
NODES = 49152


def boundary(key):
    partitions = GROUPS * OWNERS
    keys = jax.random.split(key, 13)
    scores = jax.random.randint(keys[0], (partitions, OWNERS, BLK), 0, 2 ** 20) * BLK + jnp.arange(BLK, dtype=jnp.int32)
    send_ids = jnp.argsort(scores, axis=-1)[..., :CAP].astype(jnp.int32)
    send_count = jax.random.randint(keys[1], (partitions * OWNERS,), 1, CAP + 1)
    send_count = send_count.at[jax.random.randint(keys[2], (), 0, partitions * OWNERS)].set(CAP)
    send_count = send_count.reshape(partitions, OWNERS).astype(jnp.int32)
    escores = jax.random.randint(keys[3], (partitions, 2, BLK), 0, 2 ** 20) * BLK + jnp.arange(BLK, dtype=jnp.int32)
    edge_ids = jnp.argsort(escores, axis=-1)[..., :CAPG].astype(jnp.int32)
    edge_count = jax.random.randint(keys[4], (partitions, 2), 1, CAPG + 1)
    chosen = jax.random.randint(keys[5], (), 0, partitions)
    upper = (chosen // OWNERS + 1) % GROUPS * OWNERS + chosen % OWNERS
    edge_count = edge_count.at[upper, 0].set(CAPG).astype(jnp.int32)
    shape = (partitions, BLK, TPB)
    part_ids = jnp.arange(partitions, dtype=jnp.int32)[:, None, None]
    group_of = part_ids // OWNERS
    inner_of = part_ids % OWNERS
    kinds = jax.random.randint(keys[6], shape, 0, 8)
    own_code = jax.random.randint(keys[7], shape, 0, BLK)
    offset = jax.random.randint(keys[8], shape, 1, OWNERS)
    peer_of = (inner_of + offset) % OWNERS
    peer_part = group_of * OWNERS + peer_of
    inner_slot = jax.random.randint(keys[9], shape, 0, send_count[peer_part, inner_of])
    inner_code = BLK + peer_of * CAP + inner_slot
    side_of = jax.random.randint(keys[10], shape, 0, 2)
    edge_group = jnp.where(side_of == 0, (group_of + GROUPS - 1) % GROUPS, (group_of + 1) % GROUPS)
    edge_part = edge_group * OWNERS + inner_of
    edge_slot = jax.random.randint(keys[11], shape, 0, edge_count[edge_part, 1 - side_of])
    edge_code = BLK + OWNERS * CAP + side_of * CAPG + edge_slot
    codes = jnp.where(kinds < 4, own_code, jnp.where(kinds < 6, inner_code, edge_code))
    spot = jax.random.randint(keys[12], (), 0, BLK)
    codes = codes.at[chosen, spot, 0].set(BLK + OWNERS * CAP + 2 * CAPG - 1)
    codes = codes.at[chosen, (spot + 1) % BLK, 1].set(0)
    return (send_ids, send_count, edge_ids, edge_count, codes.reshape(partitions * BLK, TPB).astype(jnp.int32))


def draw_tile_src(key, part):
    return boundary(key)[4]


def draw_send_ids(key, part):
    return boundary(key)[0]


def draw_send_count(key, part):
    return boundary(key)[1]


def draw_edge_ids(key, part):
    return boundary(key)[2]


def draw_edge_count(key, part):
    return boundary(key)[3]


def draw_adjacency(key, part):
    key = jax.random.fold_in(key, 7)
    first_key, second_key = jax.random.split(key)
    shape = (NODES, TPB * TILE)
    present = jax.random.bernoulli(first_key, 4.0 / TILE, shape)
    weights = jax.random.uniform(second_key, shape, jnp.float32, 0.5, 1.5)
    return jnp.where(present, weights, 0.0).astype(jnp.bfloat16)


def touch_ends(result, rng, low, largest):
    longest = result.shape.index(max(result.shape))
    spots = []
    for shift in (0, 1):
        where = [jax.random.randint(jax.random.fold_in(rng, axis), (), 0, length) for axis, length in enumerate(result.shape)]
        where[longest] = (where[longest] + shift) % result.shape[longest]
        spots.append(tuple(where))
    return result.at[spots[0]].set(low).at[spots[1]].set(largest)


def level_of(key, extent, cuts, least, high):
    level = 1.0
    for axis_at, shards_of in cuts:
        steps = jax.random.uniform(jax.random.fold_in(jax.random.fold_in(key, 6), axis_at), (shards_of,), jnp.float32, least / len(cuts), high / len(cuts))
        level = level * jnp.repeat(jnp.exp(steps), extent[axis_at] // shards_of).reshape((-1,) + (1,) * (len(extent) - 1 - axis_at))
    return level


def centred(key, dims, deviation, bound, cuts=(), kind=jnp.bfloat16):
    result = jax.random.normal(key, dims, jnp.float32) * deviation
    if len(cuts) > 0:
        result = level_of(key, dims, cuts, -0.22, 0.18) * result
    return jnp.clip(result, min=-bound, max=bound).astype(kind)


def setup_inputs(seed: int = 0) -> dict:
    seeds = jax.random.split(jax.random.key(seed), 11)
    features = centred(seeds[0], (NODES, F), 1.0, 6.0, ((0, 32),))
    projection = centred(seeds[1], (F, K), F ** -0.5, 0.21875)
    adjacency = draw_adjacency(jax.random.fold_in(seeds[10], 71), 0)
    degree = touch_ends(jax.random.randint(seeds[3], (NODES,), 2, 10), jax.random.fold_in(seeds[3], 1), 2, 9).astype(jnp.int32)
    tile_src = draw_tile_src(jax.random.fold_in(seeds[10], 71), 0)
    send_ids = draw_send_ids(jax.random.fold_in(seeds[10], 71), 0)
    send_count = draw_send_count(jax.random.fold_in(seeds[10], 71), 0)
    edge_ids = draw_edge_ids(jax.random.fold_in(seeds[10], 71), 0)
    edge_count = draw_edge_count(jax.random.fold_in(seeds[10], 71), 0)
    train_ids = touch_ends(jax.random.randint(seeds[9], (PARTITIONS, OWNERS, TSLOT), 0, BLK * TILE), jax.random.fold_in(seeds[9], 1), 0, (BLK * TILE) - 1).astype(jnp.int32)
    return dict(features=features, projection=projection, adjacency=adjacency, degree=degree, tile_src=tile_src, send_ids=send_ids, send_count=send_count, edge_ids=edge_ids, edge_count=edge_count, train_ids=train_ids)


def source_table(tile_src, send_ids, send_count, edge_ids, edge_count):
    partitions = GROUPS * OWNERS
    part_ids = jnp.arange(partitions, dtype=jnp.int32)[:, None, None]
    group_of = part_ids // OWNERS
    inner_of = part_ids % OWNERS
    codes = tile_src.reshape(partitions, BLK, TPB)
    inner_code = jnp.clip(codes - BLK, 0, OWNERS * CAP - 1)
    peer_of = inner_code // CAP
    inner_slot = inner_code % CAP
    inner_part = group_of * OWNERS + peer_of
    inner_block = send_ids[inner_part, inner_of, inner_slot]
    inner_live = inner_slot < send_count[inner_part, inner_of]
    edge_code = jnp.clip(codes - BLK - OWNERS * CAP, 0, 2 * CAPG - 1)
    side_of = edge_code // CAPG
    edge_slot = edge_code % CAPG
    edge_group = jnp.where(side_of == 0, (group_of + GROUPS - 1) % GROUPS, (group_of + 1) % GROUPS)
    edge_list = 1 - side_of
    edge_part = edge_group * OWNERS + inner_of
    edge_block = edge_ids[edge_part, edge_list, edge_slot]
    edge_live = edge_slot < edge_count[edge_part, edge_list]
    is_own = codes < BLK
    is_inner = jnp.logical_and(codes >= BLK, codes < BLK + OWNERS * CAP)
    owner_part = jnp.broadcast_to(part_ids, codes.shape)
    src_part = jnp.where(is_own, owner_part, jnp.where(is_inner, inner_part, edge_part))
    src_block = jnp.where(is_own, jnp.clip(codes, 0, BLK - 1), jnp.where(is_inner, inner_block, edge_block))
    src_live = jnp.where(is_own, True, jnp.where(is_inner, inner_live, edge_live))
    return (src_part.astype(jnp.int32), src_block.astype(jnp.int32), src_live)

def spread(state, adjacency, src_part, src_block, src_live):
    blocks_all = state.reshape(GROUPS * OWNERS, BLK, TILE, K)
    adj_all = adjacency.reshape(GROUPS * OWNERS, BLK, TILE, TPB * TILE)

    def one_part(item):
        adj_part, part_row, block_row, live_row = item
        fetched = blocks_all[part_row, block_row].astype(jnp.float32)
        fetched = jnp.where(live_row[:, :, None, None], fetched, jnp.zeros((), jnp.float32))
        fetched = fetched.reshape(BLK, TPB * TILE, K)
        summed = jnp.einsum('bij,bjk->bik', adj_part.astype(jnp.float32), fetched)
        return summed.reshape(BLK * TILE, K)
    return lax.map(one_part, (adj_all, src_part, src_block, src_live))

def reference(features, projection, adjacency, degree, tile_src, send_ids, send_count, edge_ids, edge_count, train_ids):
    partitions = GROUPS * OWNERS
    row_count = BLK * TILE
    inv_root = lax.rsqrt(degree.astype(jnp.float32)).reshape(partitions, row_count, 1)

    def project(item):
        feat_part, root_part = item
        product = jnp.dot(feat_part, projection, preferred_element_type=jnp.float32)
        return (root_part * product).astype(jnp.bfloat16)
    first = lax.map(project, (features.reshape(partitions, row_count, F), inv_root))
    src_part, src_block, src_live = source_table(tile_src, send_ids, send_count, edge_ids, edge_count)
    hop_one = inv_root * spread(first, adjacency, src_part, src_block, src_live)
    second = (inv_root * hop_one).astype(jnp.bfloat16)
    hop_two = inv_root * spread(second, adjacency, src_part, src_block, src_live)
    part_ids = jnp.arange(partitions, dtype=jnp.int32)[:, None, None]
    picked = jnp.concatenate([hop_one[part_ids, train_ids], hop_two[part_ids, train_ids]], axis=-1).astype(jnp.bfloat16)
    picked = picked.reshape(GROUPS, OWNERS, OWNERS, TSLOT, 2 * K).transpose(0, 2, 1, 3, 4)
    return picked.reshape(partitions * OWNERS * TSLOT, 2 * K)
```

```python
import functools

import jax
import jax.numpy as jnp
from jax import lax
from jax.experimental import pallas as pl
from jax.experimental.pallas import tpu as pltpu
from jax.sharding import PartitionSpec as P

TILE = 128
TPB = 4
CAP = 2
CAPG = 8
BF = jnp.bfloat16
F32 = jnp.float32


META = 16


def ids_row(train_ref):
    owners = train_ref.shape[1]
    return jnp.concatenate([train_ref[0, j : j + 1, :] for j in range(owners)], axis=1)


def as_columns(rows):
    return jnp.transpose(rows)


def one_hot_rows(train_ref, row_count):
    row = ids_row(train_ref)
    count = row.shape[1]
    column = as_columns(jnp.broadcast_to(row.astype(F32), (8, count)))[:, 0:1]
    lanes = lax.broadcasted_iota(jnp.int32, (count, row_count), 1)
    return (lanes == column.astype(jnp.int32)).astype(F32).astype(BF)


def root_columns(degree_ref, scratch):
    count = degree_ref.shape[0]
    scratch[...] = jnp.ones_like(scratch)
    scratch[0:count, :] = degree_ref[...].astype(F32)
    return as_columns(lax.rsqrt(scratch[...]))


def project_kernel(
    tile_src, edge_ids, send_ids, train, degree, projection, features, adjacency,
    first, off, on, *rest,
):
    inner_out, (feat, adj, degs, feat_sems, adj_sem) = rest[:-5], rest[-5:]
    blocks = first.shape[0]
    owners = train.shape[1]
    width = first.shape[2]
    count = owners * train.shape[2]
    parity = lax.rem(lax.axis_index("group"), 2)
    mine = lax.axis_index("inner")
    copies = []
    for b in range(blocks):
        copies.append(
            pltpu.make_async_copy(
                features.at[pl.ds(b * TILE, TILE)], feat.at[pl.ds(b * TILE, TILE)], feat_sems.at[b]
            )
        )
        copies[-1].start()
    adj_copy = pltpu.make_async_copy(adjacency, adj, adj_sem)
    adj_copy.start()
    roots = root_columns(degree, degs)
    weights = projection[...]
    for b in range(blocks):
        copies[b].wait()
        product = jnp.dot(feat[pl.ds(b * TILE, TILE), :], weights, preferred_element_type=F32)
        first[b] = (roots[:, b : b + 1] * product).astype(BF)
    for s in range(CAPG):
        off[pl.ds(s * TILE, TILE), :] = first[edge_ids[0, parity, s]]
        on[pl.ds(s * TILE, TILE), :] = first[edge_ids[0, 1 - parity, s]]
    for k in range(1, owners):
        peer = lax.rem(mine + k, owners)
        for s in range(CAP):
            inner_out[k - 1][pl.ds(s * TILE, TILE), :] = first[send_ids[0, peer, s]]
    row = ids_row(train)
    block_of = lax.div(row, TILE)
    lane_of = lax.rem(row, TILE)
    lane_hot = lax.broadcasted_iota(jnp.int32, (TILE, count), 0) == lane_of
    by_block = jnp.dot(degs[...].astype(BF), lane_hot.astype(F32).astype(BF), preferred_element_type=F32)
    chosen = lax.broadcasted_iota(jnp.int32, by_block.shape, 0) == block_of
    meta = [jnp.sum(jnp.where(chosen, by_block, 0.0), axis=0, keepdims=True)]
    for t in range(TPB):
        codes = jnp.zeros((1, count), F32)
        for b in range(blocks):
            codes = jnp.where(block_of == b, tile_src[b, t].astype(F32), codes)
        meta.insert(t, codes)
    meta.append(jnp.ones((META - TPB - 1, count), F32))
    meta = jnp.concatenate(meta, axis=0)
    if count < width:
        meta = jnp.concatenate([meta, jnp.ones((META, width - count), F32)], axis=1)
    meta = meta.astype(BF)
    hot = one_hot_rows(train, blocks * TILE)
    adj_copy.wait()
    picked = jnp.dot(hot, adj[...], preferred_element_type=F32).astype(BF)
    strips = TPB * TILE // width
    for target, start in [(off, CAPG * TILE), (on, CAPG * TILE)] + [(m, CAP * TILE) for m in inner_out]:
        for h in range(strips):
            target[pl.ds(start + h * count, count), :] = picked[:, h * width : (h + 1) * width]
        target[pl.ds(start + strips * count, META), :] = meta


def expanded(message, start, count, width, base, slots):
    strips = TPB * TILE // width
    columns = as_columns(message[pl.ds(start + strips * count, META), 0:count].astype(F32))
    tiles = []
    for t in range(TPB):
        h, c = divmod(t * TILE, width)
        tiles.append(message[pl.ds(start + h * count, count), c : c + TILE].astype(F32))
    parts = []
    for s in range(slots):
        want = (base + s).astype(F32) if not isinstance(base, int) else float(base + s)
        part = jnp.zeros((count, TILE), F32)
        for t in range(TPB):
            part = part + jnp.where(columns[:, t : t + 1] == want, tiles[t], 0.0)
        parts.append(part.astype(BF))
    return parts, lax.rsqrt(columns[:, TPB : TPB + 1])


def spread_kernel(
    tile_src, edge_ids, send_ids, train, degree, adjacency, first, sent, off, on, *rest,
):
    owners = train.shape[1]
    slots = train.shape[2]
    inner_in = rest[: owners - 1]
    to_off, to_on = rest[owners - 1 : owners + 1]
    stays = rest[owners + 1]
    to_inner = rest[owners + 2 : 2 * owners + 1]
    table, second, hop, degs = rest[2 * owners + 1 :]
    blocks, _, width = first.shape
    count = owners * slots
    parity = lax.rem(lax.axis_index("group"), 2)
    mine = lax.axis_index("inner")
    inner_base = blocks
    group_base = blocks + owners * CAP
    for b in range(blocks):
        table[b] = first[b]
    for s in range(CAPG):
        table[group_base + parity * CAPG + s] = off[pl.ds(s * TILE, TILE), :]
        table[group_base + (1 - parity) * CAPG + s] = on[pl.ds(s * TILE, TILE), :]
    for k in range(1, owners):
        peer = lax.rem(mine - k + owners, owners)
        for s in range(CAP):
            table[inner_base + peer * CAP + s] = inner_in[k - 1][pl.ds(s * TILE, TILE), :]
    roots = root_columns(degree, degs)
    for b in range(blocks):
        fetched = jnp.concatenate([table[tile_src[b, t]] for t in range(TPB)], axis=0)
        total = jnp.dot(adjacency[pl.ds(b * TILE, TILE), :], fetched, preferred_element_type=F32)
        root = roots[:, b : b + 1]
        one = root * total
        hop[pl.ds(b * TILE, TILE), :] = one.astype(BF)
        second[b] = (root * one).astype(BF)

    def partial(message, start, base, ids):
        parts, scale = expanded(message, start, count, width, base, len(ids))
        total = jnp.dot(
            jnp.concatenate(parts, axis=1),
            jnp.concatenate([second[i] for i in ids], axis=0),
            preferred_element_type=F32,
        )
        return (scale * total).astype(BF)

    def spread_out(target, value):
        for j in range(owners):
            target[lax.rem(j - mine + owners, owners)] = value[j * slots : (j + 1) * slots]

    spread_out(
        to_off,
        partial(off, CAPG * TILE, group_base + (1 - parity) * CAPG, [edge_ids[0, parity, s] for s in range(CAPG)]),
    )
    spread_out(
        to_on,
        partial(on, CAPG * TILE, group_base + parity * CAPG, [edge_ids[0, 1 - parity, s] for s in range(CAPG)]),
    )
    own = partial(sent, CAPG * TILE, 0, list(range(blocks)))
    picked = jnp.dot(one_hot_rows(train, blocks * TILE), hop[...], preferred_element_type=F32).astype(BF)
    values = [(mine, own), (owners, picked)]
    for k in range(1, owners):
        peer = lax.rem(mine - k + owners, owners)
        values.append(
            (peer, partial(inner_in[k - 1], CAP * TILE, inner_base + mine * CAP, [send_ids[0, peer, s] for s in range(CAP)]))
        )
    for slot, value in values:
        for k in range(owners):
            target = stays if k == 0 else to_inner[k - 1]
            owner = lax.rem(mine + k, owners)
            piece = value[0:slots]
            for j in range(1, owners):
                piece = jnp.where(owner == j, value[j * slots : (j + 1) * slots].astype(F32), piece.astype(F32)).astype(BF)
            target[slot] = piece


def gather_kernel(owners, *refs):
    stays = refs[0]
    inner = refs[:owners]
    offs = refs[owners : 2 * owners]
    ons = refs[2 * owners : 3 * owners]
    out = refs[-1]
    slots, width = stays.shape[1:]
    mine = lax.axis_index("inner")
    for k in range(owners):
        part = lax.rem(mine - k + owners, owners)
        total = offs[k][...].astype(F32) + ons[k][...].astype(F32)
        for d in range(owners):
            total = total + inner[d][part].astype(F32)
        rows = pl.ds(pl.multiple_of(part * slots, slots), slots)
        out[rows, 0:width] = inner[k][owners]
        out[rows, width : 2 * width] = total.astype(BF)


SMEM = pl.BlockSpec(memory_space=pltpu.SMEM)
VMEM = pl.BlockSpec(memory_space=pltpu.VMEM)
ANY = pl.BlockSpec(memory_space=pl.ANY)


def on_device(groups, owners, features, projection, adjacency, degree, tile_src, send_ids, edge_ids, train_ids):
    row_count, depth = features.shape
    blocks = row_count // TILE
    width = projection.shape[1]
    slots = train_ids.shape[2]
    count = owners * slots
    request = TPB * TILE // width * count + META
    degree = degree.reshape(blocks, TILE)
    params = pltpu.CompilerParams(vmem_limit_bytes=30 * 1024 * 1024)

    across = [(g, (g + (1 if g % 2 else -1)) % groups) for g in range(groups)]
    beside = [(g, g ^ 1) for g in range(groups)]

    def to(pairs, k):
        return [
            (g * owners + i, h * owners + (i + k) % owners) for g, h in pairs for i in range(owners)
        ]

    def send(value, pairs, k=0):
        if k == 0:
            return lax.ppermute(value, "group", pairs)
        return lax.ppermute(value, ("group", "inner"), to(pairs, k))

    def around(value, k):
        return lax.ppermute(value, "inner", [(i, (i + k) % owners) for i in range(owners)])

    group_message = jax.ShapeDtypeStruct((CAPG * TILE + request, width), BF)
    inner_message = jax.ShapeDtypeStruct((CAP * TILE + request, width), BF)
    first, off, on, *inner_out = pl.pallas_call(
        project_kernel,
        out_shape=[jax.ShapeDtypeStruct((blocks, TILE, width), BF), group_message, group_message]
        + [inner_message] * (owners - 1),
        in_specs=[SMEM, SMEM, SMEM, VMEM, VMEM, VMEM, ANY, ANY],
        out_specs=[VMEM] * (3 + owners - 1),
        scratch_shapes=[
            pltpu.VMEM((row_count, depth), BF),
            pltpu.VMEM((row_count, TPB * TILE), BF),
            pltpu.VMEM((16, TILE), F32),
            pltpu.SemaphoreType.DMA((blocks,)),
            pltpu.SemaphoreType.DMA,
        ],
        compiler_params=params,
        name="project",
    )(tile_src, edge_ids, send_ids, train_ids, degree, projection, features, adjacency)

    off_in = send(off, across)
    inner_in = [around(inner_out[k - 1], k) for k in range(1, owners)]
    on_in = send(on, beside)

    piece = jax.ShapeDtypeStruct((owners, slots, width), BF)
    bundle = jax.ShapeDtypeStruct((owners + 1, slots, width), BF)
    to_off, to_on, stays, *to_inner = pl.pallas_call(
        spread_kernel,
        out_shape=[piece, piece] + [bundle] * owners,
        in_specs=[SMEM, SMEM, SMEM] + [VMEM] * (7 + owners - 1),
        out_specs=[VMEM] * (2 + owners),
        scratch_shapes=[
            pltpu.VMEM((blocks + owners * CAP + 2 * CAPG, TILE, width), BF),
            pltpu.VMEM((blocks, TILE, width), BF),
            pltpu.VMEM((row_count, width), BF),
            pltpu.VMEM((16, TILE), F32),
        ],
        compiler_params=params,
        name="spread",
    )(tile_src, edge_ids, send_ids, train_ids, degree, adjacency, first, on, off_in, on_in, *inner_in)

    offs = [send(to_off[k], across, k) for k in range(owners)]
    inner = [stays] + [around(to_inner[k - 1], k) for k in range(1, owners)]
    ons = [send(to_on[k], beside, k) for k in range(owners)]
    return pl.pallas_call(
        functools.partial(gather_kernel, owners),
        out_shape=jax.ShapeDtypeStruct((count, 2 * width), BF),
        in_specs=[VMEM] * (3 * owners),
        out_specs=VMEM,
        compiler_params=params,
        name="gather",
    )(*inner, *offs, *ons)


def solution(mesh):
    both = ("group", "inner")

    def run(
        features, projection, adjacency, degree, tile_src, send_ids, send_count, edge_ids, edge_count, train_ids
    ):
        return on_device(
            mesh.shape["group"], mesh.shape["inner"],
            features, projection, adjacency, degree, tile_src, send_ids, edge_ids, train_ids,
        )

    placed = (
        P(both, None),
        P(),
        P(both, None),
        P(both),
        P(both, None),
        P(both, None, None),
        P(both, None),
        P(both, None, None),
        P(both, None),
        P(both, None, None),
    )
    return jax.shard_map(run, mesh=mesh, in_specs=placed, out_specs=P(both, None), check_vma=False)
```

```python
import functools

import jax
import jax.numpy as jnp
from jax import lax
from jax.experimental import pallas as pl
from jax.experimental.pallas import tpu as pltpu
from jax.sharding import PartitionSpec as P

TILE = 128
TPB = 4
CAP = 2
CAPG = 8
BF = jnp.bfloat16
F32 = jnp.float32
CHUNKS = 4


META = 16


def ids_row(train):
    owners = train.shape[1]
    return jnp.concatenate([train[0, j : j + 1, :] for j in range(owners)], axis=1)


def as_columns(rows):
    return jnp.transpose(rows)


def one_hot_rows(train, row_count):
    row = ids_row(train)
    count = row.shape[1]
    column = as_columns(jnp.broadcast_to(row.astype(F32), (8, count)))[:, 0:1]
    lanes = lax.broadcasted_iota(jnp.int32, (count, row_count), 1)
    return (lanes == column.astype(jnp.int32)).astype(F32).astype(BF)


def fetch(pairs, sems):
    copies = [pltpu.make_async_copy(source, target, sems.at[n]) for n, (source, target) in enumerate(pairs)]
    for copy in copies:
        copy.start()
    return copies


def project_kernel(
    tile_src, edge_ids, send_ids, train, degree, projection, features, adjacency,
    first, request, off, on, *rest,
):
    inner_out = rest[:-13]
    src_s, edge_s, send_s, train_v, deg_v, weights, feat, adj, blocks_v, request_v, sems, sent, block_sent = rest[-13:]
    blocks = first.shape[0]
    owners = train.shape[1]
    width = first.shape[2]
    count = owners * train.shape[2]
    parity = lax.rem(lax.axis_index("group"), 2)
    mine = lax.axis_index("inner")
    step = blocks // CHUNKS
    rows = [pl.ds(n * step * TILE, step * TILE) for n in range(CHUNKS)]
    small = fetch(
        [(train, train_v), (tile_src, src_s), (degree, deg_v.at[pl.ds(0, blocks)]), (edge_ids, edge_s), (send_ids, send_s)]
        + [(adjacency, adj), (projection, weights)]
        + [(features.at[r], feat.at[r]) for r in rows],
        sems,
    )
    deg_v[pl.ds(blocks, 16 - blocks), :] = jnp.ones((16 - blocks, TILE), jnp.int32)
    for copy in small[:5]:
        copy.wait()
    degrees = deg_v[...].astype(F32)
    roots = as_columns(lax.rsqrt(degrees))
    row = ids_row(train_v)
    block_of = lax.div(row, TILE)
    lane_of = lax.rem(row, TILE)
    lane_hot = lax.broadcasted_iota(jnp.int32, (TILE, count), 0) == lane_of
    by_block = jnp.dot(degrees.astype(BF), lane_hot.astype(F32).astype(BF), preferred_element_type=F32)
    chosen = lax.broadcasted_iota(jnp.int32, by_block.shape, 0) == block_of
    meta = []
    for t in range(TPB):
        codes = jnp.zeros((1, count), F32)
        for b in range(blocks):
            codes = jnp.where(block_of == b, src_s[t, b].astype(F32), codes)
        meta.append(codes)
    meta.append(jnp.sum(jnp.where(chosen, by_block, 0.0), axis=0, keepdims=True))
    meta.append(jnp.ones((META - TPB - 1, count), F32))
    meta = jnp.concatenate(meta, axis=0)
    if count < width:
        meta = jnp.concatenate([meta, jnp.ones((META, width - count), F32)], axis=1)
    strips = TPB * TILE // width
    request_v[pl.ds(strips * count, META), :] = meta.astype(BF)
    hot = one_hot_rows(train_v, blocks * TILE)
    small[5].wait()
    picked = jnp.dot(hot, adj[...], preferred_element_type=F32).astype(BF)
    for h in range(strips):
        request_v[pl.ds(h * count, count), :] = picked[:, h * width : (h + 1) * width]
    tail = request_v.shape[0]
    places = [off.at[pl.ds(CAPG * TILE, tail)]]
    places += [m.at[pl.ds(CAP * TILE, tail)] for m in inner_out]
    places += [on.at[pl.ds(CAPG * TILE, tail)], request]
    leaving = [pltpu.make_async_copy(request_v, place, sent.at[n]) for n, place in enumerate(places)]
    for copy in leaving:
        copy.start()
    offers = [(edge_s[0, parity, s], off, s) for s in range(CAPG)]
    for k in range(1, owners):
        peer = lax.rem(mine + k, owners)
        offers += [(send_s[0, peer, s], inner_out[k - 1], s) for s in range(CAP)]
    offers += [(edge_s[0, 1 - parity, s], on, s) for s in range(CAPG)]
    copies = [
        pltpu.make_async_copy(
            blocks_v.at[block], target.at[pl.ds(s * TILE, TILE)], sent.at[len(leaving) + n]
        )
        for n, (block, target, s) in enumerate(offers)
    ]
    small[6].wait()
    for n in range(CHUNKS):
        small[7 + n].wait()
        product = jnp.dot(feat[rows[n], :], weights[...], preferred_element_type=F32)
        for k in range(step):
            b = n * step + k
            blocks_v[b] = (roots[:, b : b + 1] * product[k * TILE : (k + 1) * TILE]).astype(BF)
        for copy, (block, _, _) in zip(copies, offers):
            pl.when(lax.div(block, step) == n)(copy.start)
        chunk = pl.ds(n * step, step)
        leaving.append(pltpu.make_async_copy(blocks_v.at[chunk], first.at[chunk], block_sent.at[n]))
        leaving[-1].start()
    for copy in copies + leaving:
        copy.wait()


def request_columns(message, start, count, width):
    strips = TPB * TILE // width
    return as_columns(message[pl.ds(start + strips * count, META), 0:count].astype(F32))


def expanded(message, start, count, width, wanted):
    columns = request_columns(message, start, count, width)
    tiles = []
    for t in range(TPB):
        h, c = divmod(t * TILE, width)
        tiles.append(message[pl.ds(start + h * count, count), c : c + TILE].astype(F32))
    parts = []
    for want in wanted:
        part = jnp.zeros((count, TILE), F32)
        for t in range(TPB):
            part = part + jnp.where(columns[:, t : t + 1] == want, tiles[t], 0.0)
        parts.append(part.astype(BF))
    return parts


def near_kernel(
    tile_src, edge_ids, send_ids, train, degree, first, adjacency, request, on, *rest,
):
    owners = train.shape[1]
    inner_in = rest[: owners - 1]
    sums, far, wide, hot, roots = rest[owners - 1 : owners + 4]
    src_s, edge_s, send_s, train_v, deg_v, table, sems = rest[owners + 4 :]
    blocks, _, width = first.shape
    count = owners * train.shape[2]
    parity = lax.rem(lax.axis_index("group"), 2)
    mine = lax.axis_index("inner")
    inner_base = blocks
    group_base = blocks + owners * CAP
    off_base = group_base + parity * CAPG
    on_base = group_base + (1 - parity) * CAPG
    small = fetch(
        [(train, train_v), (tile_src, src_s), (degree, deg_v.at[pl.ds(0, blocks)]), (edge_ids, edge_s), (send_ids, send_s)]
        + [(first, table.at[pl.ds(0, blocks)])],
        sems,
    )
    deg_v[pl.ds(blocks, 16 - blocks), :] = jnp.ones((16 - blocks, TILE), jnp.int32)
    far[...] = jnp.zeros_like(far)
    wide[...] = jnp.zeros_like(wide)
    for s in range(CAPG):
        table[off_base + s] = jnp.zeros((TILE, width), BF)
        table[on_base + s] = on[pl.ds(s * TILE, TILE), :]
    for s in range(CAP):
        table[inner_base + mine * CAP + s] = jnp.zeros((TILE, width), BF)
        for k in range(1, owners):
            peer = lax.rem(mine - k + owners, owners)
            table[inner_base + peer * CAP + s] = inner_in[k - 1][pl.ds(s * TILE, TILE), :]
    for copy in small:
        copy.wait()
    roots[...] = as_columns(lax.rsqrt(deg_v[...].astype(F32)))
    for b in range(blocks):
        fetched = jnp.concatenate([table[src_s[t, b]] for t in range(TPB)], axis=0)
        sums[pl.ds(b * TILE, TILE), :] = jnp.dot(
            adjacency[pl.ds(b * TILE, TILE), :], fetched, preferred_element_type=F32
        )
    for b in range(blocks):
        for t in range(TPB):
            slot = src_s[t, b] - off_base

            @pl.when(jnp.logical_and(slot >= 0, slot < CAPG))
            def _():
                place = (pl.ds(b * TILE, TILE), pl.ds(pl.multiple_of(slot * TILE, TILE), TILE))
                far[place] += adjacency[pl.ds(b * TILE, TILE), t * TILE : (t + 1) * TILE]

    parts = expanded(request, 0, count, width, [float(b) for b in range(blocks)])
    for b in range(blocks):
        wide[pl.ds(0, count), b * TILE : (b + 1) * TILE] = parts[b]
    asked = [(on, CAPG, off_base, lambda s: edge_s[0, 1 - parity, s])]
    for k in range(1, owners):
        peer = lax.rem(mine - k + owners, owners)
        asked.append((inner_in[k - 1], CAP, inner_base + mine * CAP, lambda s, peer=peer: send_s[0, peer, s]))
    for n, (message, slots, base, block) in enumerate(asked):
        parts = expanded(message, slots * TILE, count, width, [(base + s).astype(F32) for s in range(slots)])
        for s in range(slots):
            column = pl.multiple_of(block(s) * TILE, TILE)
            wide[pl.ds((n + 1) * count, count), pl.ds(column, TILE)] = parts[s]
    hot[...] = one_hot_rows(train_v, blocks * TILE)


def spread_kernel(edge_ids, off, request, on, *rest):
    owners = (len(rest) - 13) // 2 + 1
    inner_in = rest[: owners - 1]
    sums, far, wide, hot, roots = rest[owners - 1 : owners + 4]
    to_off, to_on, own, picked, *peers = rest[owners + 4 : -4]
    edge_s, second, hop, sem = rest[-4:]
    blocks = second.shape[0]
    width = second.shape[2]
    count = hot.shape[0]
    parity = lax.rem(lax.axis_index("group"), 2)
    group_base = blocks + owners * CAP
    copy = pltpu.make_async_copy(edge_ids, edge_s, sem)
    copy.start()
    step = blocks // CHUNKS
    for n in range(CHUNKS):
        rows = pl.ds(n * step * TILE, step * TILE)
        total = sums[rows, :] + jnp.dot(far[rows, :], off[pl.ds(0, CAPG * TILE), :], preferred_element_type=F32)
        for k in range(step):
            b = n * step + k
            root = roots[:, b : b + 1]
            one = root * total[k * TILE : (k + 1) * TILE]
            hop[pl.ds(b * TILE, TILE), :] = one.astype(BF)
            second[b] = (root * one).astype(BF)

    def scale(message, start):
        return lax.rsqrt(request_columns(message, start, count, width)[:, TPB : TPB + 1])

    wanted = [(group_base + (1 - parity) * CAPG + s).astype(F32) for s in range(CAPG)]
    asked = jnp.concatenate(expanded(off, CAPG * TILE, count, width, wanted), axis=1)
    copy.wait()
    offered = jnp.concatenate([second[edge_s[0, parity, s]] for s in range(CAPG)], axis=0)
    total = jnp.dot(asked, offered, preferred_element_type=F32)
    to_off[...] = (scale(off, CAPG * TILE) * total).astype(BF)
    mine = jnp.concatenate([second[b] for b in range(blocks)], axis=0)
    total = jnp.dot(wide[...], mine, preferred_element_type=F32)
    own[...] = scale(request, 0) * total[0:count]
    to_on[...] = (scale(on, CAPG * TILE) * total[count : 2 * count]).astype(BF)
    for k in range(1, owners):
        part = total[(k + 1) * count : (k + 2) * count]
        peers[k - 1][...] = (scale(inner_in[k - 1], CAP * TILE) * part).astype(BF)
    picked[...] = jnp.dot(hot[...], hop[...], preferred_element_type=F32).astype(BF)


def merge_kernel(owners, off, on, own, picked, *rest):
    peers = rest[: owners - 1]
    bundles = rest[owners - 1 :]
    slots = bundles[0].shape[1]
    mine = lax.axis_index("inner")
    for k in range(owners):
        rows = pl.ds(pl.multiple_of(lax.rem(mine + k, owners) * slots, slots), slots)
        total = own[rows, :] + off[rows, :].astype(F32) + on[rows, :].astype(F32)
        bundles[k][0] = total.astype(BF)
        bundles[k][1] = picked[rows, :]
        for r in range(1, owners):
            bundles[k][1 + r] = peers[r - 1][rows, :]


def gather_kernel(owners, *refs):
    bundles, out = refs[:owners], refs[owners]
    slots, width = bundles[0].shape[1:]
    mine = lax.axis_index("inner")
    for p in range(owners):
        total = bundles[p][0].astype(F32)
        for k in range(owners):
            if k != p:
                total = total + bundles[k][1 + (p - k) % owners].astype(F32)
        part = lax.rem(mine - p + owners, owners)
        rows = pl.ds(pl.multiple_of(part * slots, slots), slots)
        out[rows, 0:width] = bundles[p][1]
        out[rows, width : 2 * width] = total.astype(BF)


VMEM = pl.BlockSpec(memory_space=pltpu.VMEM)
HBM = pl.BlockSpec(memory_space=pltpu.HBM)


def call(kernel, name, inputs, specs, outputs, scratch=(), flops=0, limit=30, out_spec=VMEM):
    moved = sum(x.size * x.dtype.itemsize for x in list(inputs) + list(outputs))
    return pl.pallas_call(
        kernel,
        out_shape=outputs,
        in_specs=specs,
        out_specs=[out_spec] * len(outputs),
        scratch_shapes=list(scratch),
        compiler_params=pltpu.CompilerParams(vmem_limit_bytes=limit * 1024 * 1024),
        cost_estimate=pl.CostEstimate(flops=flops, bytes_accessed=moved, transcendentals=0),
        name=name,
    )(*inputs)


def on_device(groups, owners, features, projection, adjacency, degree, tile_src, send_ids, edge_ids, train_ids):
    row_count, depth = features.shape
    blocks = row_count // TILE
    width = projection.shape[1]
    slots = train_ids.shape[2]
    count = owners * slots
    request = TPB * TILE // width * count + META
    degree = degree.reshape(blocks, TILE)
    tile_src = tile_src.T
    across = [(g, (g + (1 if g % 2 else -1)) % groups) for g in range(groups)]
    beside = [(g, g ^ 1) for g in range(groups)]

    def around(value, k):
        return lax.ppermute(value, "inner", [(i, (i + k) % owners) for i in range(owners)])

    def array(*shape, kind=BF):
        return jax.ShapeDtypeStruct(shape, kind)

    integers = [
        pltpu.SMEM(tile_src.shape, jnp.int32),
        pltpu.SMEM(edge_ids.shape, jnp.int32),
        pltpu.SMEM(send_ids.shape, jnp.int32),
        pltpu.VMEM(train_ids.shape, jnp.int32),
        pltpu.VMEM((16, TILE), jnp.int32),
    ]
    indices = (tile_src, edge_ids, send_ids, train_ids, degree)
    group_message = array(CAPG * TILE + request, width)
    inner_message = array(CAP * TILE + request, width)
    first, own_request, off, on, *inner_out = call(
        project_kernel,
        "project",
        (*indices, projection, features, adjacency),
        [HBM] * 8,
        [array(blocks, TILE, width), array(request, width), group_message, group_message]
        + [inner_message] * (owners - 1),
        integers
        + [
            pltpu.VMEM(projection.shape, BF),
            pltpu.VMEM((row_count, depth), BF),
            pltpu.VMEM((row_count, TPB * TILE), BF),
            pltpu.VMEM((blocks, TILE, width), BF),
            pltpu.VMEM((request, width), BF),
            pltpu.SemaphoreType.DMA((7 + CHUNKS,)),
            pltpu.SemaphoreType.DMA((2 + owners + 2 * CAPG + (owners - 1) * CAP,)),
            pltpu.SemaphoreType.DMA((CHUNKS,)),
        ],
        2 * row_count * depth * width,
        60,
        HBM,
    )
    off_in = lax.ppermute(off, "group", across)
    inner_in = [around(inner_out[k - 1], k) for k in range(1, owners)]
    on_in = lax.ppermute(on, "group", beside)

    held = call(
        near_kernel,
        "near",
        (*indices, first, adjacency, own_request, on_in, *inner_in),
        [HBM] * 6 + [VMEM] * (2 + owners),
        [
            array(row_count, width, kind=F32),
            array(row_count, CAPG * TILE),
            array((owners + 1) * count, row_count),
            array(count, row_count),
            array(TILE, 16, kind=F32),
        ],
        integers
        + [
            pltpu.VMEM((blocks + owners * CAP + 2 * CAPG, TILE, width), BF),
            pltpu.SemaphoreType.DMA((6,)),
        ],
        2 * row_count * TPB * TILE * width,
    )
    to_off, to_on, own, picked, *peers = call(
        spread_kernel,
        "spread",
        (edge_ids, off_in, own_request, on_in, *inner_in, *held),
        [HBM] + [VMEM] * (7 + owners),
        [array(count, width), array(count, width), array(count, width, kind=F32), array(count, width)]
        + [array(count, width)] * (owners - 1),
        [
            pltpu.SMEM(edge_ids.shape, jnp.int32),
            pltpu.VMEM((blocks, TILE, width), BF),
            pltpu.VMEM((row_count, width), BF),
            pltpu.SemaphoreType.DMA,
        ],
        2 * row_count * CAPG * TILE * width,
    )
    off_part = lax.ppermute(to_off, "group", across)
    on_part = lax.ppermute(to_on, "group", beside)
    bundles = call(
        functools.partial(merge_kernel, owners),
        "merge",
        (off_part, on_part, own, picked, *peers),
        [VMEM] * (3 + owners),
        [array(1 + owners, slots, width)] * owners,
    )
    bundles = [bundles[0]] + [around(bundles[k], k) for k in range(1, owners)]
    return call(
        functools.partial(gather_kernel, owners), "gather", bundles, [VMEM] * owners, [array(count, 2 * width)]
    )[0]


def solution(mesh):
    both = ("group", "inner")

    def run(
        features, projection, adjacency, degree, tile_src, send_ids, send_count, edge_ids, edge_count, train_ids
    ):
        return on_device(
            mesh.shape["group"], mesh.shape["inner"],
            features, projection, adjacency, degree, tile_src, send_ids, edge_ids, train_ids,
        )

    placed = (
        P(both, None),
        P(),
        P(both, None),
        P(both),
        P(both, None),
        P(both, None, None),
        P(both, None),
        P(both, None, None),
        P(both, None),
        P(both, None, None),
    )
    return jax.shard_map(run, mesh=mesh, in_specs=placed, out_specs=P(both, None), check_vma=False)
```

```python
import functools

import jax
import jax.numpy as jnp
from jax import lax
from jax.experimental import pallas as pl
from jax.experimental.pallas import tpu as pltpu
from jax.sharding import PartitionSpec as P

TILE = 128
TPB = 4
CAP = 2
CAPG = 8
BF = jnp.bfloat16
F32 = jnp.float32
SPREAD_CHUNKS = 2


META = 16


def ids_row(train):
    owners = train.shape[1]
    return jnp.concatenate([train[0, j : j + 1, :] for j in range(owners)], axis=1)


def as_columns(rows):
    return jnp.transpose(rows)


def spread_lanes(column):
    return jnp.broadcast_to(column, (column.shape[0], TILE)).astype(BF)


def one_hot_parts(train, blocks):
    row = ids_row(train)
    count = row.shape[1]
    column = as_columns(jnp.broadcast_to(row.astype(F32), (8, count)))[:, 0:1].astype(jnp.int32)
    lane = lax.broadcasted_iota(jnp.int32, (count, TILE), 1) == lax.rem(column, TILE)
    lane = lane.astype(F32).astype(BF)
    block = spread_lanes(lax.div(column, TILE).astype(F32))
    nothing = jnp.zeros((), BF)
    return [jnp.where(block == jnp.array(b, BF), lane, nothing) for b in range(blocks)]


def fetch(pairs, sems):
    copies = [pltpu.make_async_copy(source, target, sems.at[n]) for n, (source, target) in enumerate(pairs)]
    for copy in copies:
        copy.start()
    return copies


def fill_degrees(degrees, blocks):
    degrees[pl.ds(blocks, 16 - blocks), :] = jnp.ones((16 - blocks, TILE), jnp.int32)


def first_kernel(edge_ids, send_ids, degree, product, first, off, on, *rest):
    inner_out = rest[:-4]
    edge_s, send_s, degrees, sems = rest[-4:]
    blocks = first.shape[0]
    owners = len(inner_out) + 1
    parity = lax.rem(lax.axis_index("group"), 2)
    mine = lax.axis_index("inner")
    arriving = fetch([(degree, degrees.at[pl.ds(0, blocks)]), (edge_ids, edge_s), (send_ids, send_s)], sems)
    fill_degrees(degrees, blocks)
    arriving[0].wait()
    roots = as_columns(lax.rsqrt(degrees[...].astype(F32)))
    for b in range(blocks):
        first[b] = (roots[:, b : b + 1] * product[pl.ds(b * TILE, TILE), :]).astype(BF)
    arriving[1].wait()
    arriving[2].wait()
    for s in range(CAPG):
        off[pl.ds(s * TILE, TILE), :] = first[edge_s[0, parity, s]]
        on[pl.ds(s * TILE, TILE), :] = first[edge_s[0, 1 - parity, s]]
    for k in range(1, owners):
        peer = lax.rem(mine + k, owners)
        for s in range(CAP):
            inner_out[k - 1][pl.ds(s * TILE, TILE), :] = first[send_s[0, peer, s]]


def request_columns(request, count, width):
    strips = TPB * TILE // width
    return as_columns(request[pl.ds(strips * count, META), 0:count].astype(F32))


def request_scale(request, count, width):
    return lax.rsqrt(request_columns(request, count, width)[:, TPB : TPB + 1])


def expanded(request, count, width, wanted):
    columns = request_columns(request, count, width)
    codes = [spread_lanes(columns[:, t : t + 1]) for t in range(TPB)]
    tiles = []
    for t in range(TPB):
        h, c = divmod(t * TILE, width)
        tiles.append(request[pl.ds(h * count, count), c : c + TILE])
    nothing = jnp.zeros((), BF)
    parts = []
    for want in wanted:
        want = jnp.asarray(want, F32).astype(BF)
        parts.append(sum(jnp.where(codes[t] == want, tiles[t], nothing) for t in range(TPB)))
    return parts


def ask_kernel(
    tile_src, train, degree, after, adjacency, request, far, hot, roots, src_s, train_v, degrees, sems
):
    blocks = degree.shape[0]
    owners = train.shape[1]
    count = owners * train.shape[2]
    width = request.shape[1]
    parity = lax.rem(lax.axis_index("group"), 2)
    off_base = blocks + owners * CAP + parity * CAPG
    arriving = fetch([(train, train_v), (tile_src, src_s), (degree, degrees.at[pl.ds(0, blocks)])], sems)
    fill_degrees(degrees, blocks)
    far[...] = jnp.zeros_like(far)
    for copy in arriving:
        copy.wait()
    roots[...] = as_columns(lax.rsqrt(degrees[...].astype(F32)))
    row = ids_row(train_v)
    block_of = lax.div(row, TILE)
    lane_hot = lax.broadcasted_iota(jnp.int32, (TILE, count), 0) == lax.rem(row, TILE)
    by_block = jnp.dot(
        degrees[...].astype(F32).astype(BF), lane_hot.astype(F32).astype(BF), preferred_element_type=F32
    )
    chosen = lax.broadcasted_iota(jnp.int32, by_block.shape, 0) == block_of
    meta = []
    for t in range(TPB):
        codes = jnp.zeros((1, count), F32)
        for b in range(blocks):
            codes = jnp.where(block_of == b, src_s[t, b].astype(F32), codes)
        meta.append(codes)
    meta.append(jnp.sum(jnp.where(chosen, by_block, 0.0), axis=0, keepdims=True))
    meta.append(jnp.ones((META - TPB - 1, count), F32))
    meta = jnp.concatenate(meta, axis=0)
    if count < width:
        meta = jnp.concatenate([meta, jnp.ones((META, width - count), F32)], axis=1)
    strips = TPB * TILE // width
    request[pl.ds(strips * count, META), :] = meta.astype(BF)
    for b, part in enumerate(one_hot_parts(train_v, blocks)):
        hot[:, b * TILE : (b + 1) * TILE] = part
    picked = jnp.dot(hot[...], adjacency[...], preferred_element_type=F32).astype(BF)
    for h in range(strips):
        request[pl.ds(h * count, count), :] = picked[:, h * width : (h + 1) * width]
    for b in range(blocks):
        for t in range(TPB):
            slot = src_s[t, b] - off_base

            @pl.when(jnp.logical_and(slot >= 0, slot < CAPG))
            def _():
                place = (pl.ds(b * TILE, TILE), pl.ds(pl.multiple_of(slot * TILE, TILE), TILE))
                far[place] += adjacency[pl.ds(b * TILE, TILE), t * TILE : (t + 1) * TILE]


def near_kernel(tile_src, first, adjacency, request, on, *rest):
    owners = len(rest) - 4
    inner_in = rest[: owners - 1]
    sums, ask, src_s, table, sems = rest[owners - 1 :]
    blocks, _, width = first.shape
    parity = lax.rem(lax.axis_index("group"), 2)
    mine = lax.axis_index("inner")
    group_base = blocks + owners * CAP
    arriving = fetch([(tile_src, src_s), (first, table.at[pl.ds(0, blocks)])], sems)
    ask[...] = request[...]
    for s in range(CAPG):
        table[group_base + parity * CAPG + s] = jnp.zeros((TILE, width), BF)
        table[group_base + (1 - parity) * CAPG + s] = on[pl.ds(s * TILE, TILE), :]
    for s in range(CAP):
        table[blocks + mine * CAP + s] = jnp.zeros((TILE, width), BF)
        for k in range(1, owners):
            peer = lax.rem(mine - k + owners, owners)
            table[blocks + peer * CAP + s] = inner_in[k - 1][pl.ds(s * TILE, TILE), :]
    for copy in arriving:
        copy.wait()
    for b in range(blocks):
        fetched = jnp.concatenate([table[src_s[t, b]] for t in range(TPB)], axis=0)
        sums[pl.ds(b * TILE, TILE), :] = jnp.dot(
            adjacency[pl.ds(b * TILE, TILE), :], fetched, preferred_element_type=F32
        )


def spread_kernel(edge_ids, off, sums, far, roots, second, hop, offered, edge_s, sem):
    row_count = second.shape[0]
    parity = lax.rem(lax.axis_index("group"), 2)
    copy = pltpu.make_async_copy(edge_ids, edge_s, sem)
    copy.start()
    chunk = row_count // SPREAD_CHUNKS
    for n in range(SPREAD_CHUNKS):
        rows = pl.ds(n * chunk, chunk)
        total = sums[rows, :] + jnp.dot(far[rows, :], off[...], preferred_element_type=F32)
        for k in range(chunk // TILE):
            b = n * (chunk // TILE) + k
            root = roots[:, b : b + 1]
            one = root * total[k * TILE : (k + 1) * TILE]
            hop[pl.ds(b * TILE, TILE), :] = one.astype(BF)
            second[pl.ds(b * TILE, TILE), :] = (root * one).astype(BF)
    copy.wait()
    for s in range(CAPG):
        block = pl.ds(pl.multiple_of(edge_s[0, parity, s] * TILE, TILE), TILE)
        offered[pl.ds(s * TILE, TILE), :] = second[block, :]


def rest_kernel(edge_ids, send_ids, second, hop, hot, request, on, *rest):
    owners = send_ids.shape[1]
    inner_in = rest[: owners - 1]
    to_on, own, picked, *peers = rest[owners - 1 : -4]
    wide, edge_s, send_s, sems = rest[-4:]
    count = hot.shape[0]
    row_count, width = second.shape
    blocks = row_count // TILE
    parity = lax.rem(lax.axis_index("group"), 2)
    mine = lax.axis_index("inner")
    arriving = fetch([(edge_ids, edge_s), (send_ids, send_s)], sems)
    wide[...] = jnp.zeros_like(wide)
    parts = expanded(request, count, width, [float(b) for b in range(blocks)])
    for b in range(blocks):
        wide[pl.ds(0, count), b * TILE : (b + 1) * TILE] = parts[b]
    picked[...] = jnp.dot(hot[...], hop[...], preferred_element_type=F32).astype(BF)
    for copy in arriving:
        copy.wait()
    asked = [(on, CAPG, blocks + owners * CAP + parity * CAPG, lambda s: edge_s[0, 1 - parity, s])]
    for k in range(1, owners):
        peer = lax.rem(mine - k + owners, owners)
        asked.append((inner_in[k - 1], CAP, blocks + mine * CAP, lambda s, peer=peer: send_s[0, peer, s]))
    for n, (message, slots, base, block) in enumerate(asked):
        parts = expanded(message, count, width, [base + s for s in range(slots)])
        for s in range(slots):
            column = pl.multiple_of(block(s) * TILE, TILE)
            wide[pl.ds((n + 1) * count, count), pl.ds(column, TILE)] = parts[s]
    total = jnp.dot(wide[...], second[...], preferred_element_type=F32)
    own[...] = request_scale(request, count, width) * total[0:count]
    to_on[...] = (request_scale(on, count, width) * total[count : 2 * count]).astype(BF)
    for k in range(1, owners):
        part = total[(k + 1) * count : (k + 2) * count]
        peers[k - 1][...] = (request_scale(inner_in[k - 1], count, width) * part).astype(BF)


def answer_kernel(group_base, request, offered, to_off):
    count, width = to_off.shape
    parity = lax.rem(lax.axis_index("group"), 2)
    base = group_base + (1 - parity) * CAPG
    asked = jnp.concatenate(expanded(request, count, width, [base + s for s in range(CAPG)]), axis=1)
    total = jnp.dot(asked, offered[...], preferred_element_type=F32)
    to_off[...] = (request_scale(request, count, width) * total).astype(BF)


def merge_kernel(owners, off, on, own, picked, *rest):
    peers = rest[: owners - 1]
    bundles = rest[owners - 1 :]
    slots = bundles[0].shape[1]
    mine = lax.axis_index("inner")
    for k in range(owners):
        rows = pl.ds(pl.multiple_of(lax.rem(mine + k, owners) * slots, slots), slots)
        total = own[rows, :] + off[rows, :].astype(F32) + on[rows, :].astype(F32)
        bundles[k][0] = total.astype(BF)
        bundles[k][1] = picked[rows, :]
        for r in range(1, owners):
            bundles[k][1 + r] = peers[r - 1][rows, :]


def gather_kernel(owners, *refs):
    bundles, out = refs[:owners], refs[owners]
    slots, width = bundles[0].shape[1:]
    mine = lax.axis_index("inner")
    for p in range(owners):
        total = bundles[p][0].astype(F32)
        for k in range(owners):
            if k != p:
                total = total + bundles[k][1 + (p - k) % owners].astype(F32)
        part = lax.rem(mine - p + owners, owners)
        rows = pl.ds(pl.multiple_of(part * slots, slots), slots)
        out[rows, 0:width] = bundles[p][1]
        out[rows, width : 2 * width] = total.astype(BF)


VMEM = pl.BlockSpec(memory_space=pltpu.VMEM)
HBM = pl.BlockSpec(memory_space=pltpu.HBM)
ANY = pl.BlockSpec(memory_space=pl.ANY)


def call(kernel, name, inputs, specs, outputs, scratch=()):
    return pl.pallas_call(
        kernel,
        out_shape=outputs,
        in_specs=specs,
        out_specs=[VMEM] * len(outputs),
        scratch_shapes=list(scratch),
        compiler_params=pltpu.CompilerParams(vmem_limit_bytes=30 * 1024 * 1024),
        name=name,
    )(*inputs)


def on_device(groups, owners, features, projection, adjacency, degree, tile_src, send_ids, edge_ids, train_ids):
    row_count, depth = features.shape
    blocks = row_count // TILE
    width = projection.shape[1]
    slots = train_ids.shape[2]
    count = owners * slots
    tail = TPB * TILE // width * count + META
    degree = degree.reshape(blocks, TILE)
    tile_src = tile_src.T
    across = [(g, (g + (1 if g % 2 else -1)) % groups) for g in range(groups)]
    beside = [(g, g ^ 1) for g in range(groups)]

    def around(value, k):
        return lax.ppermute(value, "inner", [(i, (i + k) % owners) for i in range(owners)])

    def array(*shape, kind=BF):
        return jax.ShapeDtypeStruct(shape, kind)

    def smem(like):
        return pltpu.SMEM(like.shape, jnp.int32)

    train_scratch = pltpu.VMEM(train_ids.shape, jnp.int32)
    degree_scratch = pltpu.VMEM((16, TILE), jnp.int32)
    dma = pltpu.SemaphoreType.DMA

    product = jnp.dot(features, projection, preferred_element_type=F32)
    first, off, on, *inner_out = call(
        first_kernel,
        "first",
        (edge_ids, send_ids, degree, product),
        [HBM] * 3 + [VMEM],
        [array(blocks, TILE, width), array(CAPG * TILE, width), array(CAPG * TILE, width)]
        + [array(CAP * TILE, width)] * (owners - 1),
        [smem(edge_ids), smem(send_ids), degree_scratch, dma((3,))],
    )
    off_in = lax.ppermute(off, "group", across)
    inner_in = [around(inner_out[k - 1], k) for k in range(1, owners)]
    on_in = lax.ppermute(on, "group", beside)
    request, far, hot, roots = call(
        ask_kernel,
        "ask",
        (tile_src, train_ids, degree, on_in, adjacency),
        [HBM] * 3 + [ANY, VMEM],
        [
            array(tail, width),
            array(row_count, CAPG * TILE),
            array(count, row_count),
            array(TILE, 16, kind=F32),
        ],
        [smem(tile_src), train_scratch, degree_scratch, dma((3,))],
    )
    asked_inner = [around(request, k) for k in range(1, owners)]
    asked_on = lax.ppermute(request, "group", beside)
    sums, ask = call(
        near_kernel,
        "near",
        (tile_src, first, adjacency, request, on_in, *inner_in),
        [HBM] * 2 + [VMEM] * (2 + owners),
        [array(row_count, width, kind=F32), array(tail, width)],
        [smem(tile_src), pltpu.VMEM((blocks + owners * CAP + 2 * CAPG, TILE, width), BF), dma((2,))],
    )
    asked_off = lax.ppermute(ask, "group", across)
    second, hop, offered = call(
        spread_kernel,
        "spread",
        (edge_ids, off_in, sums, far, roots),
        [HBM] + [VMEM] * 4,
        [array(row_count, width), array(row_count, width), array(CAPG * TILE, width)],
        [smem(edge_ids), dma],
    )
    (to_off,) = call(
        functools.partial(answer_kernel, blocks + owners * CAP),
        "answer",
        (asked_off, offered),
        [VMEM] * 2,
        [array(count, width)],
    )
    to_on, own, picked, *peers = call(
        rest_kernel,
        "rest",
        (edge_ids, send_ids, second, hop, hot, request, asked_on, *asked_inner),
        [HBM] * 2 + [VMEM] * (4 + owners),
        [array(count, width), array(count, width, kind=F32), array(count, width)]
        + [array(count, width)] * (owners - 1),
        [pltpu.VMEM(((owners + 1) * count, row_count), BF), smem(edge_ids), smem(send_ids), dma((2,))],
    )
    off_part = lax.ppermute(to_off, "group", across)
    on_part = lax.ppermute(to_on, "group", beside)
    bundles = call(
        functools.partial(merge_kernel, owners),
        "merge",
        (off_part, on_part, own, picked, *peers),
        [VMEM] * (3 + owners),
        [array(1 + owners, slots, width)] * owners,
    )
    bundles = [bundles[0]] + [around(bundles[k], k) for k in range(1, owners)]
    return call(
        functools.partial(gather_kernel, owners), "gather", bundles, [VMEM] * owners, [array(count, 2 * width)]
    )[0]


def solution(mesh):
    both = ("group", "inner")

    def run(
        features, projection, adjacency, degree, tile_src, send_ids, send_count, edge_ids, edge_count, train_ids
    ):
        return on_device(
            mesh.shape["group"], mesh.shape["inner"],
            features, projection, adjacency, degree, tile_src, send_ids, edge_ids, train_ids,
        )

    placed = (
        P(both, None),
        P(),
        P(both, None),
        P(both),
        P(both, None),
        P(both, None, None),
        P(both, None),
        P(both, None, None),
        P(both, None),
        P(both, None, None),
    )
    return jax.shard_map(run, mesh=mesh, in_specs=placed, out_specs=P(both, None), check_vma=False)
```

```python
import functools

import jax
import jax.numpy as jnp
from jax import lax
from jax.experimental import pallas as pl
from jax.experimental.pallas import tpu as pltpu
from jax.sharding import PartitionSpec as P

TILE = 128
TPB = 4
CAP = 2
CAPG = 8
BF = jnp.bfloat16
F32 = jnp.float32
SPREAD_CHUNKS = 3


META = 16


def ids_row(train):
    owners = train.shape[1]
    return jnp.concatenate([train[0, j : j + 1, :] for j in range(owners)], axis=1)


def as_columns(rows):
    return jnp.transpose(rows)


def spread_lanes(column):
    return jnp.broadcast_to(column, (column.shape[0], TILE)).astype(BF)


def one_hot_parts(train, blocks):
    row = ids_row(train)
    count = row.shape[1]
    column = as_columns(jnp.broadcast_to(row.astype(F32), (8, count)))[:, 0:1].astype(jnp.int32)
    lane = lax.broadcasted_iota(jnp.int32, (count, TILE), 1) == lax.rem(column, TILE)
    lane = lane.astype(F32).astype(BF)
    block = spread_lanes(lax.div(column, TILE).astype(F32))
    nothing = jnp.zeros((), BF)
    return [jnp.where(block == jnp.array(b, BF), lane, nothing) for b in range(blocks)]


def fetch(pairs, sems):
    copies = [pltpu.make_async_copy(source, target, sems.at[n]) for n, (source, target) in enumerate(pairs)]
    for copy in copies:
        copy.start()
    return copies


def fill_degrees(degrees, blocks):
    degrees[pl.ds(blocks, 16 - blocks), :] = jnp.ones((16 - blocks, TILE), jnp.int32)


def first_kernel(edge_ids, send_ids, degree, low, high, first, off, on, *rest):
    inner_out = rest[:-4]
    edge_s, send_s, degrees, sems = rest[-4:]
    blocks = first.shape[0]
    owners = len(inner_out) + 1
    parity = lax.rem(lax.axis_index("group"), 2)
    mine = lax.axis_index("inner")
    arriving = fetch([(edge_ids, edge_s), (send_ids, send_s), (degree, degrees.at[pl.ds(0, blocks)])], sems)
    fill_degrees(degrees, blocks)
    arriving[2].wait()
    roots = as_columns(lax.rsqrt(degrees[...].astype(F32)))
    for part, rows in ((low, 0), (high, low.shape[0] // TILE)):
        for b in range(part.shape[0] // TILE):
            root = roots[:, rows + b : rows + b + 1]
            first[rows + b] = (root * part[pl.ds(b * TILE, TILE), :]).astype(BF)
    arriving[0].wait()
    arriving[1].wait()
    for s in range(CAPG):
        off[pl.ds(s * TILE, TILE), :] = first[edge_s[0, parity, s]]
        on[pl.ds(s * TILE, TILE), :] = first[edge_s[0, 1 - parity, s]]
    for k in range(1, owners):
        peer = lax.rem(mine + k, owners)
        for s in range(CAP):
            inner_out[k - 1][pl.ds(s * TILE, TILE), :] = first[send_s[0, peer, s]]


def request_columns(request, count, width):
    strips = TPB * TILE // width
    return as_columns(request[pl.ds(strips * count, META), 0:count].astype(F32))


def request_scale(request, count, width):
    return lax.rsqrt(request_columns(request, count, width)[:, TPB : TPB + 1])


def expanded(request, count, width, wanted):
    columns = request_columns(request, count, width)
    codes = [spread_lanes(columns[:, t : t + 1]) for t in range(TPB)]
    tiles = []
    for t in range(TPB):
        h, c = divmod(t * TILE, width)
        tiles.append(request[pl.ds(h * count, count), c : c + TILE])
    nothing = jnp.zeros((), BF)
    parts = []
    for want in wanted:
        want = jnp.asarray(want, F32).astype(BF)
        parts.append(sum(jnp.where(codes[t] == want, tiles[t], nothing) for t in range(TPB)))
    return parts


def ask_kernel(tile_src, train, degree, after, adjacency, request, src_s, train_v, degrees, sems):
    blocks = degree.shape[0]
    owners = train.shape[1]
    count = owners * train.shape[2]
    width = request.shape[1]
    arriving = fetch([(train, train_v), (tile_src, src_s), (degree, degrees.at[pl.ds(0, blocks)])], sems)
    fill_degrees(degrees, blocks)
    arriving[0].wait()
    hot = jnp.concatenate(one_hot_parts(train_v, blocks), axis=1)
    picked = jnp.dot(hot, adjacency[...], preferred_element_type=F32).astype(BF)
    strips = TPB * TILE // width
    for h in range(strips):
        request[pl.ds(h * count, count), :] = picked[:, h * width : (h + 1) * width]
    arriving[1].wait()
    arriving[2].wait()
    row = ids_row(train_v)
    block_of = lax.div(row, TILE)
    lane_hot = lax.broadcasted_iota(jnp.int32, (TILE, count), 0) == lax.rem(row, TILE)
    by_block = jnp.dot(
        degrees[...].astype(F32).astype(BF), lane_hot.astype(F32).astype(BF), preferred_element_type=F32
    )
    chosen = lax.broadcasted_iota(jnp.int32, by_block.shape, 0) == block_of
    meta = []
    for t in range(TPB):
        codes = jnp.zeros((1, count), F32)
        for b in range(blocks):
            codes = jnp.where(block_of == b, src_s[t, b].astype(F32), codes)
        meta.append(codes)
    meta.append(jnp.sum(jnp.where(chosen, by_block, 0.0), axis=0, keepdims=True))
    meta.append(jnp.ones((META - TPB - 1, count), F32))
    meta = jnp.concatenate(meta, axis=0)
    if count < width:
        meta = jnp.concatenate([meta, jnp.ones((META, width - count), F32)], axis=1)
    request[pl.ds(strips * count, META), :] = meta.astype(BF)


def far_kernel(
    tile_src, train, degree, adjacency, request, far, hot, roots, wide, src_s, train_v, degrees, sems
):
    blocks = degree.shape[0]
    owners = train.shape[1]
    parity = lax.rem(lax.axis_index("group"), 2)
    off_base = blocks + owners * CAP + parity * CAPG
    arriving = fetch([(train, train_v), (tile_src, src_s), (degree, degrees.at[pl.ds(0, blocks)])], sems)
    fill_degrees(degrees, blocks)
    far[...] = jnp.zeros_like(far)
    count, width = hot.shape[0], request.shape[1]
    for b, part in enumerate(expanded(request, count, width, [float(b) for b in range(blocks)])):
        wide[:, b * TILE : (b + 1) * TILE] = part
    for copy in arriving:
        copy.wait()
    roots[...] = as_columns(lax.rsqrt(degrees[...].astype(F32)))
    for b, part in enumerate(one_hot_parts(train_v, blocks)):
        hot[:, b * TILE : (b + 1) * TILE] = part
    for b in range(blocks):
        for t in range(TPB):
            slot = src_s[t, b] - off_base

            @pl.when(jnp.logical_and(slot >= 0, slot < CAPG))
            def _():
                place = (pl.ds(b * TILE, TILE), pl.ds(pl.multiple_of(slot * TILE, TILE), TILE))
                far[place] += adjacency[pl.ds(b * TILE, TILE), t * TILE : (t + 1) * TILE]


def near_kernel(tile_src, first, adjacency, request, on, *rest):
    owners = len(rest) - 4
    inner_in = rest[: owners - 1]
    sums, ask, src_s, table, sems = rest[owners - 1 :]
    blocks, _, width = first.shape
    parity = lax.rem(lax.axis_index("group"), 2)
    mine = lax.axis_index("inner")
    group_base = blocks + owners * CAP
    arriving = fetch([(tile_src, src_s), (first, table.at[pl.ds(0, blocks)])], sems)
    ask[...] = request[...]
    for s in range(CAPG):
        table[group_base + parity * CAPG + s] = jnp.zeros((TILE, width), BF)
        table[group_base + (1 - parity) * CAPG + s] = on[pl.ds(s * TILE, TILE), :]
    for s in range(CAP):
        table[blocks + mine * CAP + s] = jnp.zeros((TILE, width), BF)
        for k in range(1, owners):
            peer = lax.rem(mine - k + owners, owners)
            table[blocks + peer * CAP + s] = inner_in[k - 1][pl.ds(s * TILE, TILE), :]
    for copy in arriving:
        copy.wait()
    for b in range(blocks):
        fetched = jnp.concatenate([table[src_s[t, b]] for t in range(TPB)], axis=0)
        sums[pl.ds(b * TILE, TILE), :] = jnp.dot(
            adjacency[pl.ds(b * TILE, TILE), :], fetched, preferred_element_type=F32
        )


def spread_kernel(edge_ids, off, sums, far, roots, second, hop, offered, offered_on, edge_s, sem):
    row_count = second.shape[0]
    parity = lax.rem(lax.axis_index("group"), 2)
    copy = pltpu.make_async_copy(edge_ids, edge_s, sem)
    copy.start()
    chunk = row_count // SPREAD_CHUNKS
    for n in range(SPREAD_CHUNKS):
        rows = pl.ds(n * chunk, chunk)
        total = sums[rows, :] + jnp.dot(far[rows, :], off[...], preferred_element_type=F32)
        for k in range(chunk // TILE):
            b = n * (chunk // TILE) + k
            root = roots[:, b : b + 1]
            one = root * total[k * TILE : (k + 1) * TILE]
            hop[pl.ds(b * TILE, TILE), :] = one.astype(BF)
            second[pl.ds(b * TILE, TILE), :] = (root * one).astype(BF)
    copy.wait()
    for s in range(CAPG):
        block = pl.ds(pl.multiple_of(edge_s[0, parity, s] * TILE, TILE), TILE)
        offered[pl.ds(s * TILE, TILE), :] = second[block, :]
        block = pl.ds(pl.multiple_of(edge_s[0, 1 - parity, s] * TILE, TILE), TILE)
        offered_on[pl.ds(s * TILE, TILE), :] = second[block, :]


def rest_kernel(send_ids, second, hop, hot, wide, request, *rest):
    owners = send_ids.shape[1]
    inner_in = rest[: owners - 1]
    own, picked, *peers = rest[owners - 1 : -2]
    send_s, sem = rest[-2:]
    count = hot.shape[0]
    row_count, width = second.shape
    blocks = row_count // TILE
    mine = lax.axis_index("inner")
    copy = pltpu.make_async_copy(send_ids, send_s, sem)
    copy.start()
    total = jnp.dot(wide[...], second[...], preferred_element_type=F32)
    own[...] = request_scale(request, count, width) * total
    picked[...] = jnp.dot(hot[...], hop[...], preferred_element_type=F32).astype(BF)
    copy.wait()
    for k in range(1, owners):
        peer = lax.rem(mine - k + owners, owners)
        message = inner_in[k - 1]
        base = blocks + mine * CAP
        asked = jnp.concatenate(expanded(message, count, width, [base + s for s in range(CAP)]), axis=1)
        offered = [
            second[pl.ds(pl.multiple_of(send_s[0, peer, s] * TILE, TILE), TILE), :] for s in range(CAP)
        ]
        total = jnp.dot(asked, jnp.concatenate(offered, axis=0), preferred_element_type=F32)
        peers[k - 1][...] = (request_scale(message, count, width) * total).astype(BF)


def answer_kernel(group_base, off, offered, on, offered_on, to_off, to_on):
    count, width = to_off.shape
    parity = lax.rem(lax.axis_index("group"), 2)
    for request, rows, base, answer in (
        (off, offered, group_base + (1 - parity) * CAPG, to_off),
        (on, offered_on, group_base + parity * CAPG, to_on),
    ):
        asked = jnp.concatenate(expanded(request, count, width, [base + s for s in range(CAPG)]), axis=1)
        total = jnp.dot(asked, rows[...], preferred_element_type=F32)
        answer[...] = (request_scale(request, count, width) * total).astype(BF)


def merge_kernel(owners, off, on, own, picked, *rest):
    peers = rest[: owners - 1]
    bundles = rest[owners - 1 :]
    slots = bundles[0].shape[1]
    mine = lax.axis_index("inner")
    for k in range(owners):
        rows = pl.ds(pl.multiple_of(lax.rem(mine + k, owners) * slots, slots), slots)
        total = own[rows, :] + off[rows, :].astype(F32) + on[rows, :].astype(F32)
        bundles[k][0] = total.astype(BF)
        bundles[k][1] = picked[rows, :]
        for r in range(1, owners):
            bundles[k][1 + r] = peers[r - 1][rows, :]


def gather_kernel(owners, *refs):
    bundles, out = refs[:owners], refs[owners]
    slots, width = bundles[0].shape[1:]
    mine = lax.axis_index("inner")
    for p in range(owners):
        total = bundles[p][0].astype(F32)
        for k in range(owners):
            if k != p:
                total = total + bundles[k][1 + (p - k) % owners].astype(F32)
        part = lax.rem(mine - p + owners, owners)
        rows = pl.ds(pl.multiple_of(part * slots, slots), slots)
        out[rows, 0:width] = bundles[p][1]
        out[rows, width : 2 * width] = total.astype(BF)


VMEM = pl.BlockSpec(memory_space=pltpu.VMEM)
HBM = pl.BlockSpec(memory_space=pltpu.HBM)
ANY = pl.BlockSpec(memory_space=pl.ANY)


def call(kernel, name, inputs, specs, outputs, scratch=()):
    return pl.pallas_call(
        kernel,
        out_shape=outputs,
        in_specs=specs,
        out_specs=[VMEM] * len(outputs),
        scratch_shapes=list(scratch),
        compiler_params=pltpu.CompilerParams(vmem_limit_bytes=30 * 1024 * 1024),
        name=name,
    )(*inputs)


def on_device(groups, owners, features, projection, adjacency, degree, tile_src, send_ids, edge_ids, train_ids):
    row_count, depth = features.shape
    blocks = row_count // TILE
    width = projection.shape[1]
    slots = train_ids.shape[2]
    count = owners * slots
    tail = TPB * TILE // width * count + META
    degree = degree.reshape(blocks, TILE)
    tile_src = tile_src.T
    across = [(g, (g + (1 if g % 2 else -1)) % groups) for g in range(groups)]
    beside = [(g, g ^ 1) for g in range(groups)]

    def around(value, k):
        return lax.ppermute(value, "inner", [(i, (i + k) % owners) for i in range(owners)])

    def array(*shape, kind=BF):
        return jax.ShapeDtypeStruct(shape, kind)

    def smem(like):
        return pltpu.SMEM(like.shape, jnp.int32)

    train_scratch = pltpu.VMEM(train_ids.shape, jnp.int32)
    degree_scratch = pltpu.VMEM((16, TILE), jnp.int32)
    dma = pltpu.SemaphoreType.DMA

    cut = row_count // 2
    low, high = [
        jnp.dot(features[r], projection, preferred_element_type=F32) for r in (slice(0, cut), slice(cut, row_count))
    ]
    first, off, on, *inner_out = call(
        first_kernel,
        "first",
        (edge_ids, send_ids, degree, low, high),
        [HBM] * 3 + [VMEM] * 2,
        [array(blocks, TILE, width), array(CAPG * TILE, width), array(CAPG * TILE, width)]
        + [array(CAP * TILE, width)] * (owners - 1),
        [smem(edge_ids), smem(send_ids), degree_scratch, dma((3,))],
    )
    off_in = lax.ppermute(off, "group", across)
    inner_in = [around(inner_out[k - 1], k) for k in range(1, owners)]
    on_in = lax.ppermute(on, "group", beside)
    (request,) = call(
        ask_kernel,
        "ask",
        (tile_src, train_ids, degree, first, adjacency),
        [HBM] * 3 + [ANY, VMEM],
        [array(tail, width)],
        [smem(tile_src), train_scratch, degree_scratch, dma((3,))],
    )
    asked_off = lax.ppermute(request, "group", across)
    far, hot, roots, wide = call(
        far_kernel,
        "far",
        (tile_src, train_ids, degree, adjacency, request),
        [HBM] * 3 + [VMEM] * 2,
        [
            array(row_count, CAPG * TILE),
            array(count, row_count),
            array(TILE, 16, kind=F32),
            array(count, row_count),
        ],
        [smem(tile_src), train_scratch, degree_scratch, dma((3,))],
    )
    sums, ask = call(
        near_kernel,
        "near",
        (tile_src, first, adjacency, request, on_in, *inner_in),
        [HBM] * 2 + [VMEM] * (2 + owners),
        [array(row_count, width, kind=F32), array(tail, width)],
        [smem(tile_src), pltpu.VMEM((blocks + owners * CAP + 2 * CAPG, TILE, width), BF), dma((2,))],
    )
    asked_on = lax.ppermute(ask, "group", beside)
    asked_inner = [around(ask, k) for k in range(1, owners)]
    second, hop, offered, offered_on = call(
        spread_kernel,
        "spread",
        (edge_ids, off_in, sums, far, roots),
        [HBM] + [VMEM] * 4,
        [array(row_count, width)] * 2 + [array(CAPG * TILE, width)] * 2,
        [smem(edge_ids), dma],
    )
    to_off, to_on = call(
        functools.partial(answer_kernel, blocks + owners * CAP),
        "answer",
        (asked_off, offered, asked_on, offered_on),
        [VMEM] * 4,
        [array(count, width)] * 2,
    )
    own, picked, *peers = call(
        rest_kernel,
        "rest",
        (send_ids, second, hop, hot, wide, request, *asked_inner),
        [HBM] + [VMEM] * (4 + owners),
        [array(count, width, kind=F32)] + [array(count, width)] * owners,
        [smem(send_ids), dma],
    )
    off_part = lax.ppermute(to_off, "group", across)
    on_part = lax.ppermute(to_on, "group", beside)
    bundles = call(
        functools.partial(merge_kernel, owners),
        "merge",
        (off_part, on_part, own, picked, *peers),
        [VMEM] * (3 + owners),
        [array(1 + owners, slots, width)] * owners,
    )
    bundles = [bundles[0]] + [around(bundles[k], k) for k in range(1, owners)]
    return call(
        functools.partial(gather_kernel, owners), "gather", bundles, [VMEM] * owners, [array(count, 2 * width)]
    )[0]


def solution(mesh):
    both = ("group", "inner")

    def run(
        features, projection, adjacency, degree, tile_src, send_ids, send_count, edge_ids, edge_count, train_ids
    ):
        return on_device(
            mesh.shape["group"], mesh.shape["inner"],
            features, projection, adjacency, degree, tile_src, send_ids, edge_ids, train_ids,
        )

    placed = (
        P(both, None),
        P(),
        P(both, None),
        P(both),
        P(both, None),
        P(both, None, None),
        P(both, None),
        P(both, None, None),
        P(both, None),
        P(both, None, None),
    )
    return jax.shard_map(run, mesh=mesh, in_specs=placed, out_specs=P(both, None), check_vma=False)
```

```python
import functools

import jax
import jax.numpy as jnp
from jax import lax
from jax.experimental import pallas as pl
from jax.experimental.pallas import tpu as pltpu
from jax.sharding import PartitionSpec as P

TILE = 128
TPB = 4
CAP = 2
CAPG = 8
BF = jnp.bfloat16
F32 = jnp.float32
SPREAD_CHUNKS = 3


META = 16


def ids_row(train):
    owners = train.shape[1]
    return jnp.concatenate([train[0, j : j + 1, :] for j in range(owners)], axis=1)


def as_columns(rows):
    return jnp.transpose(rows)


def spread_lanes(column):
    return jnp.broadcast_to(column, (column.shape[0], TILE)).astype(BF)


def one_hot_parts(train, blocks):
    row = ids_row(train)
    count = row.shape[1]
    column = as_columns(jnp.broadcast_to(row.astype(F32), (8, count)))[:, 0:1].astype(jnp.int32)
    lane = lax.broadcasted_iota(jnp.int32, (count, TILE), 1) == lax.rem(column, TILE)
    lane = lane.astype(F32).astype(BF)
    block = spread_lanes(lax.div(column, TILE).astype(F32))
    nothing = jnp.zeros((), BF)
    return [jnp.where(block == jnp.array(b, BF), lane, nothing) for b in range(blocks)]


def fetch(pairs, sems):
    copies = [pltpu.make_async_copy(source, target, sems.at[n]) for n, (source, target) in enumerate(pairs)]
    for copy in copies:
        copy.start()
    return copies


def fill_degrees(degrees, blocks):
    degrees[pl.ds(blocks, 16 - blocks), :] = jnp.ones((16 - blocks, TILE), jnp.int32)


def first_kernel(edge_ids, send_ids, degree, projection, features, head, first, off, on, *rest):
    inner_out = rest[:-4]
    edge_s, send_s, degrees, sems = rest[-4:]
    blocks = first.shape[0]
    owners = len(inner_out) + 1
    parity = lax.rem(lax.axis_index("group"), 2)
    mine = lax.axis_index("inner")
    arriving = fetch([(edge_ids, edge_s), (send_ids, send_s), (degree, degrees.at[pl.ds(0, blocks)])], sems)
    fill_degrees(degrees, blocks)
    arriving[2].wait()
    roots = as_columns(lax.rsqrt(degrees[...].astype(F32)))
    done = head.shape[0] // TILE
    for b in range(done):
        first[b] = (roots[:, b : b + 1] * head[pl.ds(b * TILE, TILE), :]).astype(BF)
    product = jnp.dot(
        features[pl.ds(done * TILE, (blocks - done) * TILE), :], projection[...], preferred_element_type=F32
    )
    for b in range(done, blocks):
        first[b] = (roots[:, b : b + 1] * product[(b - done) * TILE : (b - done + 1) * TILE]).astype(BF)
    arriving[0].wait()
    arriving[1].wait()
    for s in range(CAPG):
        off[pl.ds(s * TILE, TILE), :] = first[edge_s[0, parity, s]]
        on[pl.ds(s * TILE, TILE), :] = first[edge_s[0, 1 - parity, s]]
    for k in range(1, owners):
        peer = lax.rem(mine + k, owners)
        for s in range(CAP):
            inner_out[k - 1][pl.ds(s * TILE, TILE), :] = first[send_s[0, peer, s]]


def request_columns(request, count, width):
    strips = TPB * TILE // width
    return as_columns(request[pl.ds(strips * count, META), 0:count].astype(F32))


def request_scale(request, count, width):
    return lax.rsqrt(request_columns(request, count, width)[:, TPB : TPB + 1])


def expanded(request, count, width, wanted):
    columns = request_columns(request, count, width)
    codes = [spread_lanes(columns[:, t : t + 1]) for t in range(TPB)]
    tiles = []
    for t in range(TPB):
        h, c = divmod(t * TILE, width)
        tiles.append(request[pl.ds(h * count, count), c : c + TILE])
    nothing = jnp.zeros((), BF)
    parts = []
    for want in wanted:
        want = jnp.asarray(want, F32).astype(BF)
        parts.append(sum(jnp.where(codes[t] == want, tiles[t], nothing) for t in range(TPB)))
    return parts


def ask_kernel(tile_src, train, degree, after, adjacency, request, src_s, train_v, degrees, sems):
    blocks = degree.shape[0]
    owners = train.shape[1]
    count = owners * train.shape[2]
    width = request.shape[1]
    arriving = fetch([(train, train_v), (tile_src, src_s), (degree, degrees.at[pl.ds(0, blocks)])], sems)
    fill_degrees(degrees, blocks)
    arriving[0].wait()
    hot = jnp.concatenate(one_hot_parts(train_v, blocks), axis=1)
    picked = jnp.dot(hot, adjacency[...], preferred_element_type=F32).astype(BF)
    strips = TPB * TILE // width
    for h in range(strips):
        request[pl.ds(h * count, count), :] = picked[:, h * width : (h + 1) * width]
    arriving[1].wait()
    arriving[2].wait()
    row = ids_row(train_v)
    block_of = lax.div(row, TILE)
    lane_hot = lax.broadcasted_iota(jnp.int32, (TILE, count), 0) == lax.rem(row, TILE)
    by_block = jnp.dot(
        degrees[...].astype(F32).astype(BF), lane_hot.astype(F32).astype(BF), preferred_element_type=F32
    )
    chosen = lax.broadcasted_iota(jnp.int32, by_block.shape, 0) == block_of
    meta = []
    for t in range(TPB):
        codes = jnp.zeros((1, count), F32)
        for b in range(blocks):
            codes = jnp.where(block_of == b, src_s[t, b].astype(F32), codes)
        meta.append(codes)
    meta.append(jnp.sum(jnp.where(chosen, by_block, 0.0), axis=0, keepdims=True))
    meta.append(jnp.ones((META - TPB - 1, count), F32))
    meta = jnp.concatenate(meta, axis=0)
    if count < width:
        meta = jnp.concatenate([meta, jnp.ones((META, width - count), F32)], axis=1)
    request[pl.ds(strips * count, META), :] = meta.astype(BF)


def far_kernel(
    tile_src, train, degree, adjacency, request, far, hot, roots, wide, ask, src_s, train_v, degrees, sems
):
    blocks = degree.shape[0]
    owners = train.shape[1]
    parity = lax.rem(lax.axis_index("group"), 2)
    off_base = blocks + owners * CAP + parity * CAPG
    arriving = fetch([(train, train_v), (tile_src, src_s), (degree, degrees.at[pl.ds(0, blocks)])], sems)
    fill_degrees(degrees, blocks)
    far[...] = jnp.zeros_like(far)
    count, width = hot.shape[0], request.shape[1]
    ask[...] = request[...]
    for b, part in enumerate(expanded(request, count, width, [float(b) for b in range(blocks)])):
        wide[:, b * TILE : (b + 1) * TILE] = part
    for copy in arriving:
        copy.wait()
    roots[...] = as_columns(lax.rsqrt(degrees[...].astype(F32)))
    for b, part in enumerate(one_hot_parts(train_v, blocks)):
        hot[:, b * TILE : (b + 1) * TILE] = part
    for b in range(blocks):
        for t in range(TPB):
            slot = src_s[t, b] - off_base

            @pl.when(jnp.logical_and(slot >= 0, slot < CAPG))
            def _():
                place = (pl.ds(b * TILE, TILE), pl.ds(pl.multiple_of(slot * TILE, TILE), TILE))
                far[place] += adjacency[pl.ds(b * TILE, TILE), t * TILE : (t + 1) * TILE]


def near_kernel(tile_src, first, adjacency, request, on, *rest):
    owners = len(rest) - 4
    inner_in = rest[: owners - 1]
    sums, ask, src_s, table, sems = rest[owners - 1 :]
    blocks, _, width = first.shape
    parity = lax.rem(lax.axis_index("group"), 2)
    mine = lax.axis_index("inner")
    group_base = blocks + owners * CAP
    arriving = fetch([(tile_src, src_s), (first, table.at[pl.ds(0, blocks)])], sems)
    ask[...] = request[...]
    for s in range(CAPG):
        table[group_base + parity * CAPG + s] = jnp.zeros((TILE, width), BF)
        table[group_base + (1 - parity) * CAPG + s] = on[pl.ds(s * TILE, TILE), :]
    for s in range(CAP):
        table[blocks + mine * CAP + s] = jnp.zeros((TILE, width), BF)
        for k in range(1, owners):
            peer = lax.rem(mine - k + owners, owners)
            table[blocks + peer * CAP + s] = inner_in[k - 1][pl.ds(s * TILE, TILE), :]
    for copy in arriving:
        copy.wait()
    for b in range(blocks):
        fetched = jnp.concatenate([table[src_s[t, b]] for t in range(TPB)], axis=0)
        sums[pl.ds(b * TILE, TILE), :] = jnp.dot(
            adjacency[pl.ds(b * TILE, TILE), :], fetched, preferred_element_type=F32
        )


def spread_kernel(edge_ids, off, sums, far, roots, second, hop, offered, offered_on, edge_s, sem):
    row_count = second.shape[0]
    parity = lax.rem(lax.axis_index("group"), 2)
    copy = pltpu.make_async_copy(edge_ids, edge_s, sem)
    copy.start()
    chunk = row_count // SPREAD_CHUNKS
    for n in range(SPREAD_CHUNKS):
        rows = pl.ds(n * chunk, chunk)
        total = sums[rows, :] + jnp.dot(far[rows, :], off[...], preferred_element_type=F32)
        for k in range(chunk // TILE):
            b = n * (chunk // TILE) + k
            root = roots[:, b : b + 1]
            one = root * total[k * TILE : (k + 1) * TILE]
            hop[pl.ds(b * TILE, TILE), :] = one.astype(BF)
            second[pl.ds(b * TILE, TILE), :] = (root * one).astype(BF)
    copy.wait()
    for s in range(CAPG):
        block = pl.ds(pl.multiple_of(edge_s[0, parity, s] * TILE, TILE), TILE)
        offered[pl.ds(s * TILE, TILE), :] = second[block, :]
        block = pl.ds(pl.multiple_of(edge_s[0, 1 - parity, s] * TILE, TILE), TILE)
        offered_on[pl.ds(s * TILE, TILE), :] = second[block, :]


def rest_kernel(send_ids, second, hop, hot, wide, request, *rest):
    owners = send_ids.shape[1]
    inner_in = rest[: owners - 1]
    own, picked, *peers = rest[owners - 1 : -2]
    send_s, sem = rest[-2:]
    count = hot.shape[0]
    row_count, width = second.shape
    blocks = row_count // TILE
    mine = lax.axis_index("inner")
    copy = pltpu.make_async_copy(send_ids, send_s, sem)
    copy.start()
    total = jnp.dot(wide[...], second[...], preferred_element_type=F32)
    own[...] = request_scale(request, count, width) * total
    picked[...] = jnp.dot(hot[...], hop[...], preferred_element_type=F32).astype(BF)
    copy.wait()
    for k in range(1, owners):
        peer = lax.rem(mine - k + owners, owners)
        message = inner_in[k - 1]
        base = blocks + mine * CAP
        asked = jnp.concatenate(expanded(message, count, width, [base + s for s in range(CAP)]), axis=1)
        offered = [
            second[pl.ds(pl.multiple_of(send_s[0, peer, s] * TILE, TILE), TILE), :] for s in range(CAP)
        ]
        total = jnp.dot(asked, jnp.concatenate(offered, axis=0), preferred_element_type=F32)
        peers[k - 1][...] = (request_scale(message, count, width) * total).astype(BF)


def answer_kernel(group_base, off, offered, on, offered_on, to_off, to_on):
    count, width = to_off.shape
    parity = lax.rem(lax.axis_index("group"), 2)
    for request, rows, base, answer in (
        (off, offered, group_base + (1 - parity) * CAPG, to_off),
        (on, offered_on, group_base + parity * CAPG, to_on),
    ):
        asked = jnp.concatenate(expanded(request, count, width, [base + s for s in range(CAPG)]), axis=1)
        total = jnp.dot(asked, rows[...], preferred_element_type=F32)
        answer[...] = (request_scale(request, count, width) * total).astype(BF)


def merge_kernel(owners, off, on, own, picked, *rest):
    peers = rest[: owners - 1]
    bundles = rest[owners - 1 :]
    slots = bundles[0].shape[1]
    mine = lax.axis_index("inner")
    for k in range(owners):
        rows = pl.ds(pl.multiple_of(lax.rem(mine + k, owners) * slots, slots), slots)
        total = own[rows, :] + off[rows, :].astype(F32) + on[rows, :].astype(F32)
        bundles[k][0] = total.astype(BF)
        bundles[k][1] = picked[rows, :]
        for r in range(1, owners):
            bundles[k][1 + r] = peers[r - 1][rows, :]


def gather_kernel(owners, *refs):
    bundles, out = refs[:owners], refs[owners]
    slots, width = bundles[0].shape[1:]
    mine = lax.axis_index("inner")
    for p in range(owners):
        total = bundles[p][0].astype(F32)
        for k in range(owners):
            if k != p:
                total = total + bundles[k][1 + (p - k) % owners].astype(F32)
        part = lax.rem(mine - p + owners, owners)
        rows = pl.ds(pl.multiple_of(part * slots, slots), slots)
        out[rows, 0:width] = bundles[p][1]
        out[rows, width : 2 * width] = total.astype(BF)


VMEM = pl.BlockSpec(memory_space=pltpu.VMEM)
HBM = pl.BlockSpec(memory_space=pltpu.HBM)
ANY = pl.BlockSpec(memory_space=pl.ANY)


def call(kernel, name, inputs, specs, outputs, scratch=()):
    return pl.pallas_call(
        kernel,
        out_shape=outputs,
        in_specs=specs,
        out_specs=[VMEM] * len(outputs),
        scratch_shapes=list(scratch),
        compiler_params=pltpu.CompilerParams(vmem_limit_bytes=30 * 1024 * 1024),
        name=name,
    )(*inputs)


def on_device(groups, owners, features, projection, adjacency, degree, tile_src, send_ids, edge_ids, train_ids):
    row_count, depth = features.shape
    blocks = row_count // TILE
    width = projection.shape[1]
    slots = train_ids.shape[2]
    count = owners * slots
    tail = TPB * TILE // width * count + META
    degree = degree.reshape(blocks, TILE)
    tile_src = tile_src.T
    across = [(g, (g + (1 if g % 2 else -1)) % groups) for g in range(groups)]
    beside = [(g, g ^ 1) for g in range(groups)]

    def around(value, k):
        return lax.ppermute(value, "inner", [(i, (i + k) % owners) for i in range(owners)])

    def array(*shape, kind=BF):
        return jax.ShapeDtypeStruct(shape, kind)

    def smem(like):
        return pltpu.SMEM(like.shape, jnp.int32)

    train_scratch = pltpu.VMEM(train_ids.shape, jnp.int32)
    degree_scratch = pltpu.VMEM((16, TILE), jnp.int32)
    dma = pltpu.SemaphoreType.DMA

    head = jnp.dot(features[: blocks * 7 // 12 * TILE], projection, preferred_element_type=F32)
    first, off, on, *inner_out = call(
        first_kernel,
        "first",
        (edge_ids, send_ids, degree, projection, features, head),
        [HBM] * 3 + [VMEM] * 3,
        [array(blocks, TILE, width), array(CAPG * TILE, width), array(CAPG * TILE, width)]
        + [array(CAP * TILE, width)] * (owners - 1),
        [smem(edge_ids), smem(send_ids), degree_scratch, dma((3,))],
    )
    off_in = lax.ppermute(off, "group", across)
    inner_in = [around(inner_out[k - 1], k) for k in range(1, owners)]
    on_in = lax.ppermute(on, "group", beside)
    (request,) = call(
        ask_kernel,
        "ask",
        (tile_src, train_ids, degree, first, adjacency),
        [HBM] * 3 + [ANY, VMEM],
        [array(tail, width)],
        [smem(tile_src), train_scratch, degree_scratch, dma((3,))],
    )
    asked_off = lax.ppermute(request, "group", across)
    far, hot, roots, wide, ask = call(
        far_kernel,
        "far",
        (tile_src, train_ids, degree, adjacency, request),
        [HBM] * 3 + [VMEM] * 2,
        [
            array(row_count, CAPG * TILE),
            array(count, row_count),
            array(TILE, 16, kind=F32),
            array(count, row_count),
            array(tail, width),
        ],
        [smem(tile_src), train_scratch, degree_scratch, dma((3,))],
    )
    sums, ask = call(
        near_kernel,
        "near",
        (tile_src, first, adjacency, ask, on_in, *inner_in),
        [HBM] * 2 + [VMEM] * (2 + owners),
        [array(row_count, width, kind=F32), array(tail, width)],
        [smem(tile_src), pltpu.VMEM((blocks + owners * CAP + 2 * CAPG, TILE, width), BF), dma((2,))],
    )
    asked_on = lax.ppermute(ask, "group", beside)
    asked_inner = [around(ask, k) for k in range(1, owners)]
    second, hop, offered, offered_on = call(
        spread_kernel,
        "spread",
        (edge_ids, off_in, sums, far, roots),
        [HBM] + [VMEM] * 4,
        [array(row_count, width)] * 2 + [array(CAPG * TILE, width)] * 2,
        [smem(edge_ids), dma],
    )
    to_off, to_on = call(
        functools.partial(answer_kernel, blocks + owners * CAP),
        "answer",
        (asked_off, offered, asked_on, offered_on),
        [VMEM] * 4,
        [array(count, width)] * 2,
    )
    own, picked, *peers = call(
        rest_kernel,
        "rest",
        (send_ids, second, hop, hot, wide, request, *asked_inner),
        [HBM] + [VMEM] * (4 + owners),
        [array(count, width, kind=F32)] + [array(count, width)] * owners,
        [smem(send_ids), dma],
    )
    off_part = lax.ppermute(to_off, "group", across)
    on_part = lax.ppermute(to_on, "group", beside)
    bundles = call(
        functools.partial(merge_kernel, owners),
        "merge",
        (off_part, on_part, own, picked, *peers),
        [VMEM] * (3 + owners),
        [array(1 + owners, slots, width)] * owners,
    )
    bundles = [bundles[0]] + [around(bundles[k], k) for k in range(1, owners)]
    return call(
        functools.partial(gather_kernel, owners), "gather", bundles, [VMEM] * owners, [array(count, 2 * width)]
    )[0]


def solution(mesh):
    both = ("group", "inner")

    def run(
        features, projection, adjacency, degree, tile_src, send_ids, send_count, edge_ids, edge_count, train_ids
    ):
        return on_device(
            mesh.shape["group"], mesh.shape["inner"],
            features, projection, adjacency, degree, tile_src, send_ids, edge_ids, train_ids,
        )

    placed = (
        P(both, None),
        P(),
        P(both, None),
        P(both),
        P(both, None),
        P(both, None, None),
        P(both, None),
        P(both, None, None),
        P(both, None),
        P(both, None, None),
    )
    return jax.shard_map(run, mesh=mesh, in_specs=placed, out_specs=P(both, None), check_vma=False)
```

```python
import functools

import jax
import jax.numpy as jnp
from jax import lax
from jax.experimental import pallas as pl
from jax.experimental.pallas import tpu as pltpu
from jax.sharding import PartitionSpec as P

TILE = 128
TPB = 4
CAP = 2
CAPG = 8
BF = jnp.bfloat16
F32 = jnp.float32
SHARE = 1.0 / TPB
ON_PARTS = 2
SPREAD_CHUNKS = 3


META = 16


def ids_row(train):
    owners = train.shape[1]
    return jnp.concatenate([train[0, j : j + 1, :] for j in range(owners)], axis=1)


def as_columns(rows):
    return jnp.transpose(rows)


def spread_lanes(column):
    return jnp.broadcast_to(column, (column.shape[0], TILE)).astype(BF)


def one_hot_parts(train, blocks):
    row = ids_row(train)
    count = row.shape[1]
    column = as_columns(jnp.broadcast_to(row.astype(F32), (8, count)))[:, 0:1].astype(jnp.int32)
    lane = lax.broadcasted_iota(jnp.int32, (count, TILE), 1) == lax.rem(column, TILE)
    lane = lane.astype(F32).astype(BF)
    block = spread_lanes(lax.div(column, TILE).astype(F32))
    nothing = jnp.zeros((), BF)
    return [jnp.where(block == jnp.array(b, BF), lane, nothing) for b in range(blocks)]


def fetch(pairs, sems):
    copies = [pltpu.make_async_copy(source, target, sems.at[n]) for n, (source, target) in enumerate(pairs)]
    for copy in copies:
        copy.start()
    return copies


def fill_degrees(degree, degrees):
    degrees[...] = jnp.ones_like(degrees)
    degrees[pl.ds(0, degree.shape[0]), :] = degree[...]


def first_kernel(edge_ids, send_ids, degree, projection, features, head, first, off, *rest):
    on_parts, inner_out = rest[:ON_PARTS], rest[ON_PARTS:-4]
    edge_s, send_s, degrees, sems = rest[-4:]
    blocks = first.shape[0]
    owners = len(inner_out) + 1
    parity = lax.rem(lax.axis_index("group"), 2)
    mine = lax.axis_index("inner")
    arriving = fetch([(edge_ids, edge_s), (send_ids, send_s)], sems)
    fill_degrees(degree, degrees)
    roots = as_columns(lax.rsqrt(degrees[...].astype(F32)))
    done = head.shape[0] // TILE
    for b in range(done):
        first[b] = (roots[:, b : b + 1] * head[pl.ds(b * TILE, TILE), :]).astype(BF)
    product = jnp.dot(
        features[pl.ds(done * TILE, (blocks - done) * TILE), :], projection[...], preferred_element_type=F32
    )
    for b in range(done, blocks):
        first[b] = (roots[:, b : b + 1] * product[(b - done) * TILE : (b - done + 1) * TILE]).astype(BF)
    arriving[0].wait()
    arriving[1].wait()
    for s in range(CAPG):
        off[pl.ds(s * TILE, TILE), :] = first[edge_s[0, parity, s]]
        part, place = divmod(s, CAPG // ON_PARTS)
        on_parts[part][pl.ds(place * TILE, TILE), :] = first[edge_s[0, 1 - parity, s]]
    for k in range(1, owners):
        peer = lax.rem(mine + k, owners)
        for s in range(CAP):
            inner_out[k - 1][pl.ds(s * TILE, TILE), :] = first[send_s[0, peer, s]]


def request_columns(request, count, width):
    strips = TPB * TILE // width
    return as_columns(request[pl.ds(strips * count, META), 0:count].astype(F32))


def request_scale(request, count, width):
    return TPB * TPB * lax.rsqrt(request_columns(request, count, width)[:, TPB : TPB + 1])


def expanded(request, count, width, wanted):
    columns = request_columns(request, count, width)
    codes = [spread_lanes(columns[:, t : t + 1]) for t in range(TPB)]
    tiles = []
    for t in range(TPB):
        h, c = divmod(t * TILE, width)
        tiles.append(jnp.array(SHARE, BF) * request[pl.ds(h * count, count), c : c + TILE])
    nothing = jnp.zeros((), BF)
    parts = []
    for want in wanted:
        want = jnp.asarray(want, F32).astype(BF)
        parts.append(sum(jnp.where(codes[t] == want, tiles[t], nothing) for t in range(TPB)))
    return parts


def ask_kernel(tile_src, train, degree, after, adjacency, request, src_s, degrees, sem):
    blocks = degree.shape[0]
    owners = train.shape[1]
    count = owners * train.shape[2]
    width = request.shape[1]
    copy = pltpu.make_async_copy(tile_src, src_s, sem)
    copy.start()
    fill_degrees(degree, degrees)
    hot = jnp.concatenate(one_hot_parts(train, blocks), axis=1)
    picked = jnp.dot(hot, adjacency[...], preferred_element_type=F32).astype(BF)
    strips = TPB * TILE // width
    for h in range(strips):
        request[pl.ds(h * count, count), :] = picked[:, h * width : (h + 1) * width]
    copy.wait()
    row = ids_row(train)
    block_of = lax.div(row, TILE)
    lane_hot = lax.broadcasted_iota(jnp.int32, (TILE, count), 0) == lax.rem(row, TILE)
    by_block = jnp.dot(
        degrees[...].astype(F32).astype(BF), lane_hot.astype(F32).astype(BF), preferred_element_type=F32
    )
    chosen = lax.broadcasted_iota(jnp.int32, by_block.shape, 0) == block_of
    meta = []
    for t in range(TPB):
        codes = jnp.zeros((1, count), F32)
        for b in range(blocks):
            codes = jnp.where(block_of == b, src_s[t, b].astype(F32), codes)
        meta.append(codes)
    meta.append(jnp.sum(jnp.where(chosen, by_block, 0.0), axis=0, keepdims=True))
    meta.append(jnp.ones((META - TPB - 1, count), F32))
    meta = jnp.concatenate(meta, axis=0)
    if count < width:
        meta = jnp.concatenate([meta, jnp.ones((META, width - count), F32)], axis=1)
    request[pl.ds(strips * count, META), :] = meta.astype(BF)


def far_kernel(
    tile_src, train, degree, adjacency, request, far, hot, roots, wide, ask, src_s, degrees, sem
):
    blocks = degree.shape[0]
    owners = train.shape[1]
    parity = lax.rem(lax.axis_index("group"), 2)
    off_base = blocks + owners * CAP + parity * CAPG
    copy = pltpu.make_async_copy(tile_src, src_s, sem)
    copy.start()
    fill_degrees(degree, degrees)
    far[...] = jnp.zeros_like(far)
    share = jnp.array(SHARE, BF)
    count, width = hot.shape[0], request.shape[1]
    ask[...] = request[...]
    for b, part in enumerate(expanded(request, count, width, [float(b) for b in range(blocks)])):
        wide[:, b * TILE : (b + 1) * TILE] = part
    copy.wait()
    roots[...] = as_columns(lax.rsqrt(degrees[...].astype(F32)))
    for b, part in enumerate(one_hot_parts(train, blocks)):
        hot[:, b * TILE : (b + 1) * TILE] = part
    for b in range(blocks):
        for t in range(TPB):
            slot = src_s[t, b] - off_base

            @pl.when(jnp.logical_and(slot >= 0, slot < CAPG))
            def _():
                place = (pl.ds(b * TILE, TILE), pl.ds(pl.multiple_of(slot * TILE, TILE), TILE))
                far[place] += share * adjacency[pl.ds(b * TILE, TILE), t * TILE : (t + 1) * TILE]


def near_kernel(tile_src, first, adjacency, request, *rest):
    on, rest = rest[:ON_PARTS], rest[ON_PARTS:]
    owners = len(rest) - 4
    inner_in = rest[: owners - 1]
    sums, ask, src_s, table, sems = rest[owners - 1 :]
    blocks, _, width = first.shape
    parity = lax.rem(lax.axis_index("group"), 2)
    mine = lax.axis_index("inner")
    group_base = blocks + owners * CAP
    arriving = fetch([(tile_src, src_s), (first, table.at[pl.ds(0, blocks)])], sems)
    ask[...] = request[...]
    for s in range(CAPG):
        table[group_base + parity * CAPG + s] = jnp.zeros((TILE, width), BF)
        table[group_base + (1 - parity) * CAPG + s] = on[s // (CAPG // ON_PARTS)][pl.ds(s % (CAPG // ON_PARTS) * TILE, TILE), :]
    for s in range(CAP):
        table[blocks + mine * CAP + s] = jnp.zeros((TILE, width), BF)
        for k in range(1, owners):
            peer = lax.rem(mine - k + owners, owners)
            table[blocks + peer * CAP + s] = inner_in[k - 1][pl.ds(s * TILE, TILE), :]
    for copy in arriving:
        copy.wait()
    for b in range(blocks):
        fetched = jnp.concatenate([table[src_s[t, b]] for t in range(TPB)], axis=0)
        total = jnp.dot(adjacency[pl.ds(b * TILE, TILE), :], fetched, preferred_element_type=F32)
        sums[pl.ds(b * TILE, TILE), :] = SHARE * total


def spread_kernel(edge_ids, off, sums, far, roots, second, hop, offered, offered_on, edge_s, sem):
    row_count = second.shape[0]
    parity = lax.rem(lax.axis_index("group"), 2)
    copy = pltpu.make_async_copy(edge_ids, edge_s, sem)
    copy.start()
    chunk = row_count // SPREAD_CHUNKS
    for n in range(SPREAD_CHUNKS):
        rows = pl.ds(n * chunk, chunk)
        total = sums[rows, :] + jnp.dot(far[rows, :], off[...], preferred_element_type=F32)
        for k in range(chunk // TILE):
            b = n * (chunk // TILE) + k
            root = roots[:, b : b + 1]
            one = root * total[k * TILE : (k + 1) * TILE]
            hop[pl.ds(b * TILE, TILE), :] = one.astype(BF)
            second[pl.ds(b * TILE, TILE), :] = (root * one).astype(BF)
    copy.wait()
    for s in range(CAPG):
        block = pl.ds(pl.multiple_of(edge_s[0, parity, s] * TILE, TILE), TILE)
        offered[pl.ds(s * TILE, TILE), :] = second[block, :]
        block = pl.ds(pl.multiple_of(edge_s[0, 1 - parity, s] * TILE, TILE), TILE)
        offered_on[pl.ds(s * TILE, TILE), :] = second[block, :]


def rest_kernel(send_ids, second, hop, hot, wide, request, *rest):
    owners = send_ids.shape[1]
    inner_in = rest[: owners - 1]
    own, picked, *peers = rest[owners - 1 : -2]
    send_s, sem = rest[-2:]
    count = hot.shape[0]
    row_count, width = second.shape
    blocks = row_count // TILE
    mine = lax.axis_index("inner")
    copy = pltpu.make_async_copy(send_ids, send_s, sem)
    copy.start()
    total = jnp.dot(wide[...], second[...], preferred_element_type=F32)
    own[...] = request_scale(request, count, width) * total
    picked[...] = (TPB * jnp.dot(hot[...], hop[...], preferred_element_type=F32)).astype(BF)
    copy.wait()
    for k in range(1, owners):
        peer = lax.rem(mine - k + owners, owners)
        message = inner_in[k - 1]
        base = blocks + mine * CAP
        asked = jnp.concatenate(expanded(message, count, width, [base + s for s in range(CAP)]), axis=1)
        offered = [
            second[pl.ds(pl.multiple_of(send_s[0, peer, s] * TILE, TILE), TILE), :] for s in range(CAP)
        ]
        total = jnp.dot(asked, jnp.concatenate(offered, axis=0), preferred_element_type=F32)
        peers[k - 1][...] = (request_scale(message, count, width) * total).astype(BF)


def answer_kernel(group_base, off, offered, on, offered_on, to_off, to_on):
    count, width = to_off.shape
    parity = lax.rem(lax.axis_index("group"), 2)
    for request, rows, base, answer in (
        (off, offered, group_base + (1 - parity) * CAPG, to_off),
        (on, offered_on, group_base + parity * CAPG, to_on),
    ):
        asked = jnp.concatenate(expanded(request, count, width, [base + s for s in range(CAPG)]), axis=1)
        total = jnp.dot(asked, rows[...], preferred_element_type=F32)
        answer[...] = (request_scale(request, count, width) * total).astype(BF)


def merge_kernel(owners, off, on, own, picked, *rest):
    peers = rest[: owners - 1]
    bundles = rest[owners - 1 :]
    slots = bundles[0].shape[1]
    mine = lax.axis_index("inner")
    for k in range(owners):
        rows = pl.ds(pl.multiple_of(lax.rem(mine + k, owners) * slots, slots), slots)
        total = own[rows, :] + off[rows, :].astype(F32) + on[rows, :].astype(F32)
        bundles[k][0] = total.astype(BF)
        bundles[k][1] = picked[rows, :]
        for r in range(1, owners):
            bundles[k][1 + r] = peers[r - 1][rows, :]


def gather_kernel(owners, *refs):
    bundles, out = refs[:owners], refs[owners]
    slots, width = bundles[0].shape[1:]
    mine = lax.axis_index("inner")
    for p in range(owners):
        total = bundles[p][0].astype(F32)
        for k in range(owners):
            if k != p:
                total = total + bundles[k][1 + (p - k) % owners].astype(F32)
        part = lax.rem(mine - p + owners, owners)
        rows = pl.ds(pl.multiple_of(part * slots, slots), slots)
        out[rows, 0:width] = bundles[p][1]
        out[rows, width : 2 * width] = total.astype(BF)


VMEM = pl.BlockSpec(memory_space=pltpu.VMEM)
HBM = pl.BlockSpec(memory_space=pltpu.HBM)
ANY = pl.BlockSpec(memory_space=pl.ANY)


def call(kernel, name, inputs, specs, outputs, scratch=()):
    return pl.pallas_call(
        kernel,
        out_shape=outputs,
        in_specs=specs,
        out_specs=[VMEM] * len(outputs),
        scratch_shapes=list(scratch),
        compiler_params=pltpu.CompilerParams(vmem_limit_bytes=30 * 1024 * 1024),
        name=name,
    )(*inputs)


def on_device(groups, owners, features, projection, adjacency, degree, tile_src, send_ids, edge_ids, train_ids):
    row_count, depth = features.shape
    blocks = row_count // TILE
    width = projection.shape[1]
    slots = train_ids.shape[2]
    count = owners * slots
    tail = TPB * TILE // width * count + META
    degree = degree.reshape(blocks, TILE)
    tile_src = tile_src.T
    across = [(g, (g + (1 if g % 2 else -1)) % groups) for g in range(groups)]
    beside = [(g, g ^ 1) for g in range(groups)]

    def around(value, k):
        return lax.ppermute(value, "inner", [(i, (i + k) % owners) for i in range(owners)])

    def array(*shape, kind=BF):
        return jax.ShapeDtypeStruct(shape, kind)

    def smem(like):
        return pltpu.SMEM(like.shape, jnp.int32)

    degree_scratch = pltpu.VMEM((16, TILE), jnp.int32)
    dma = pltpu.SemaphoreType.DMA

    head = jnp.dot(features[: blocks * 7 // 12 * TILE], projection, preferred_element_type=F32)
    first, off, *outgoing = call(
        first_kernel,
        "first",
        (edge_ids, send_ids, degree, projection, features, head),
        [HBM] * 2 + [VMEM] * 4,
        [array(blocks, TILE, width), array(CAPG * TILE, width)]
        + [array(CAPG // ON_PARTS * TILE, width)] * ON_PARTS
        + [array(CAP * TILE, width)] * (owners - 1),
        [smem(edge_ids), smem(send_ids), degree_scratch, dma((2,))],
    )
    on, inner_out = outgoing[:ON_PARTS], outgoing[ON_PARTS:]
    off_in = lax.ppermute(off, "group", across)
    inner_in = [around(inner_out[k - 1], k) for k in range(1, owners)]
    on_in = [lax.ppermute(part, "group", beside) for part in on]
    (request,) = call(
        ask_kernel,
        "ask",
        (tile_src, train_ids, degree, first, adjacency),
        [HBM] + [VMEM] * 2 + [ANY, VMEM],
        [array(tail, width)],
        [smem(tile_src), degree_scratch, dma],
    )
    asked_off = lax.ppermute(request, "group", across)
    far, hot, roots, wide, ask = call(
        far_kernel,
        "far",
        (tile_src, train_ids, degree, adjacency, request),
        [HBM] + [VMEM] * 4,
        [
            array(row_count, CAPG * TILE),
            array(count, row_count),
            array(TILE, 16, kind=F32),
            array(count, row_count),
            array(tail, width),
        ],
        [smem(tile_src), degree_scratch, dma],
    )
    sums, ask = call(
        near_kernel,
        "near",
        (tile_src, first, adjacency, ask, *on_in, *inner_in),
        [HBM] * 2 + [VMEM] * (1 + ON_PARTS + owners),
        [array(row_count, width, kind=F32), array(tail, width)],
        [smem(tile_src), pltpu.VMEM((blocks + owners * CAP + 2 * CAPG, TILE, width), BF), dma((2,))],
    )
    asked_on = lax.ppermute(ask, "group", beside)
    asked_inner = [around(ask, k) for k in range(1, owners)]
    second, hop, offered, offered_on = call(
        spread_kernel,
        "spread",
        (edge_ids, off_in, sums, far, roots),
        [HBM] + [VMEM] * 4,
        [array(row_count, width)] * 2 + [array(CAPG * TILE, width)] * 2,
        [smem(edge_ids), dma],
    )
    to_off, to_on = call(
        functools.partial(answer_kernel, blocks + owners * CAP),
        "answer",
        (asked_off, offered, asked_on, offered_on),
        [VMEM] * 4,
        [array(count, width)] * 2,
    )
    own, picked, *peers = call(
        rest_kernel,
        "rest",
        (send_ids, second, hop, hot, wide, request, *asked_inner),
        [HBM] + [VMEM] * (4 + owners),
        [array(count, width, kind=F32)] + [array(count, width)] * owners,
        [smem(send_ids), dma],
    )
    off_part = lax.ppermute(to_off, "group", across)
    on_part = lax.ppermute(to_on, "group", beside)
    bundles = call(
        functools.partial(merge_kernel, owners),
        "merge",
        (off_part, on_part, own, picked, *peers),
        [VMEM] * (3 + owners),
        [array(1 + owners, slots, width)] * owners,
    )
    bundles = [bundles[0]] + [around(bundles[k], k) for k in range(1, owners)]
    return call(
        functools.partial(gather_kernel, owners), "gather", bundles, [VMEM] * owners, [array(count, 2 * width)]
    )[0]


def solution(mesh):
    both = ("group", "inner")

    def run(
        features, projection, adjacency, degree, tile_src, send_ids, send_count, edge_ids, edge_count, train_ids
    ):
        return on_device(
            mesh.shape["group"], mesh.shape["inner"],
            features, projection, adjacency, degree, tile_src, send_ids, edge_ids, train_ids,
        )

    placed = (
        P(both, None),
        P(),
        P(both, None),
        P(both),
        P(both, None),
        P(both, None, None),
        P(both, None),
        P(both, None, None),
        P(both, None),
        P(both, None, None),
    )
    return jax.shard_map(run, mesh=mesh, in_specs=placed, out_specs=P(both, None), check_vma=False)
```

```python
import functools

import jax
import jax.numpy as jnp
from jax import lax
from jax.experimental import pallas as pl
from jax.experimental.pallas import tpu as pltpu
from jax.sharding import PartitionSpec as P

TILE = 128
TPB = 4
CAP = 2
CAPG = 8
BF = jnp.bfloat16
F32 = jnp.float32
SHARE = 1.0 / TPB
ON_PARTS = 1
SPREAD_CHUNKS = 3


META = 16


def ids_row(train):
    owners = train.shape[1]
    return jnp.concatenate([train[0, j : j + 1, :] for j in range(owners)], axis=1)


def as_columns(rows):
    return jnp.transpose(rows)


def spread_lanes(column):
    return jnp.broadcast_to(column, (column.shape[0], TILE)).astype(BF)


def one_hot_parts(train, blocks):
    row = ids_row(train)
    count = row.shape[1]
    column = as_columns(jnp.broadcast_to(row.astype(F32), (8, count)))[:, 0:1].astype(jnp.int32)
    lane = lax.broadcasted_iota(jnp.int32, (count, TILE), 1) == lax.rem(column, TILE)
    lane = lane.astype(F32).astype(BF)
    block = spread_lanes(lax.div(column, TILE).astype(F32))
    nothing = jnp.zeros((), BF)
    return [jnp.where(block == jnp.array(b, BF), lane, nothing) for b in range(blocks)]


def fetch(pairs, sems):
    copies = [pltpu.make_async_copy(source, target, sems.at[n]) for n, (source, target) in enumerate(pairs)]
    for copy in copies:
        copy.start()
    return copies


def fill_degrees(degree, degrees):
    degrees[...] = jnp.ones_like(degrees)
    degrees[pl.ds(0, degree.shape[0]), :] = degree[...]


def first_kernel(edge_ids, send_ids, degree, projection, features, head, first, off, *rest):
    on_parts, inner_out = rest[:ON_PARTS], rest[ON_PARTS:-4]
    edge_s, send_s, degrees, sems = rest[-4:]
    blocks = first.shape[0]
    owners = len(inner_out) + 1
    parity = lax.rem(lax.axis_index("group"), 2)
    mine = lax.axis_index("inner")
    arriving = fetch([(edge_ids, edge_s), (send_ids, send_s)], sems)
    fill_degrees(degree, degrees)
    roots = as_columns(lax.rsqrt(degrees[...].astype(F32)))
    done = head.shape[0] // TILE
    for b in range(done):
        first[b] = (roots[:, b : b + 1] * head[pl.ds(b * TILE, TILE), :]).astype(BF)
    product = jnp.dot(
        features[pl.ds(done * TILE, (blocks - done) * TILE), :], projection[...], preferred_element_type=F32
    )
    for b in range(done, blocks):
        first[b] = (roots[:, b : b + 1] * product[(b - done) * TILE : (b - done + 1) * TILE]).astype(BF)
    arriving[0].wait()
    arriving[1].wait()
    for s in range(CAPG):
        off[pl.ds(s * TILE, TILE), :] = first[edge_s[0, parity, s]]
        part, place = divmod(s, CAPG // ON_PARTS)
        on_parts[part][pl.ds(place * TILE, TILE), :] = first[edge_s[0, 1 - parity, s]]
    for k in range(1, owners):
        peer = lax.rem(mine + k, owners)
        for s in range(CAP):
            inner_out[k - 1][pl.ds(s * TILE, TILE), :] = first[send_s[0, peer, s]]


def request_columns(request, count, width):
    strips = TPB * TILE // width
    return as_columns(request[pl.ds(strips * count, META), 0:count].astype(F32))


def request_scale(request, count, width):
    return TPB * TPB * lax.rsqrt(request_columns(request, count, width)[:, TPB : TPB + 1])


def expanded(request, count, width, wanted):
    columns = request_columns(request, count, width)
    codes = [spread_lanes(columns[:, t : t + 1]) for t in range(TPB)]
    tiles = []
    for t in range(TPB):
        h, c = divmod(t * TILE, width)
        tiles.append(jnp.array(SHARE, BF) * request[pl.ds(h * count, count), c : c + TILE])
    nothing = jnp.zeros((), BF)
    parts = []
    for want in wanted:
        want = jnp.asarray(want, F32).astype(BF)
        parts.append(sum(jnp.where(codes[t] == want, tiles[t], nothing) for t in range(TPB)))
    return parts


def ask_kernel(tile_src, train, degree, after, adjacency, request, src_s, degrees, sem):
    blocks = degree.shape[0]
    owners = train.shape[1]
    count = owners * train.shape[2]
    width = request.shape[1]
    copy = pltpu.make_async_copy(tile_src, src_s, sem)
    copy.start()
    fill_degrees(degree, degrees)
    hot = jnp.concatenate(one_hot_parts(train, blocks), axis=1)
    picked = jnp.dot(hot, adjacency[...], preferred_element_type=F32).astype(BF)
    strips = TPB * TILE // width
    for h in range(strips):
        request[pl.ds(h * count, count), :] = picked[:, h * width : (h + 1) * width]
    copy.wait()
    row = ids_row(train)
    block_of = lax.div(row, TILE)
    lane_hot = lax.broadcasted_iota(jnp.int32, (TILE, count), 0) == lax.rem(row, TILE)
    by_block = jnp.dot(
        degrees[...].astype(F32).astype(BF), lane_hot.astype(F32).astype(BF), preferred_element_type=F32
    )
    chosen = lax.broadcasted_iota(jnp.int32, by_block.shape, 0) == block_of
    meta = []
    for t in range(TPB):
        codes = jnp.zeros((1, count), F32)
        for b in range(blocks):
            codes = jnp.where(block_of == b, src_s[t, b].astype(F32), codes)
        meta.append(codes)
    meta.append(jnp.sum(jnp.where(chosen, by_block, 0.0), axis=0, keepdims=True))
    meta.append(jnp.ones((META - TPB - 1, count), F32))
    meta = jnp.concatenate(meta, axis=0)
    if count < width:
        meta = jnp.concatenate([meta, jnp.ones((META, width - count), F32)], axis=1)
    request[pl.ds(strips * count, META), :] = meta.astype(BF)


def far_kernel(
    tile_src, train, degree, adjacency, request, far, hot, roots, wide, ask, src_s, degrees, sem
):
    blocks = degree.shape[0]
    owners = train.shape[1]
    parity = lax.rem(lax.axis_index("group"), 2)
    off_base = blocks + owners * CAP + parity * CAPG
    copy = pltpu.make_async_copy(tile_src, src_s, sem)
    copy.start()
    fill_degrees(degree, degrees)
    far[...] = jnp.zeros_like(far)
    share = jnp.array(SHARE, BF)
    count, width = hot.shape[0], request.shape[1]
    ask[...] = request[...]
    for b, part in enumerate(expanded(request, count, width, [float(b) for b in range(blocks)])):
        wide[:, b * TILE : (b + 1) * TILE] = part
    copy.wait()
    roots[...] = as_columns(lax.rsqrt(degrees[...].astype(F32)))
    for b, part in enumerate(one_hot_parts(train, blocks)):
        hot[:, b * TILE : (b + 1) * TILE] = part
    for b in range(blocks):
        for t in range(TPB):
            slot = src_s[t, b] - off_base

            @pl.when(jnp.logical_and(slot >= 0, slot < CAPG))
            def _():
                place = (pl.ds(b * TILE, TILE), pl.ds(pl.multiple_of(slot * TILE, TILE), TILE))
                far[place] += share * adjacency[pl.ds(b * TILE, TILE), t * TILE : (t + 1) * TILE]


def near_kernel(tile_src, first, adjacency, request, *rest):
    on, rest = rest[:ON_PARTS], rest[ON_PARTS:]
    owners = len(rest) - 4
    inner_in = rest[: owners - 1]
    sums, ask, src_s, table, sems = rest[owners - 1 :]
    blocks, _, width = first.shape
    parity = lax.rem(lax.axis_index("group"), 2)
    mine = lax.axis_index("inner")
    group_base = blocks + owners * CAP
    arriving = fetch([(tile_src, src_s), (first, table.at[pl.ds(0, blocks)])], sems)
    ask[...] = request[...]
    for s in range(CAPG):
        table[group_base + parity * CAPG + s] = jnp.zeros((TILE, width), BF)
        table[group_base + (1 - parity) * CAPG + s] = on[s // (CAPG // ON_PARTS)][pl.ds(s % (CAPG // ON_PARTS) * TILE, TILE), :]
    for s in range(CAP):
        table[blocks + mine * CAP + s] = jnp.zeros((TILE, width), BF)
        for k in range(1, owners):
            peer = lax.rem(mine - k + owners, owners)
            table[blocks + peer * CAP + s] = inner_in[k - 1][pl.ds(s * TILE, TILE), :]
    for copy in arriving:
        copy.wait()
    for b in range(blocks):
        fetched = jnp.concatenate([table[src_s[t, b]] for t in range(TPB)], axis=0)
        total = jnp.dot(adjacency[pl.ds(b * TILE, TILE), :], fetched, preferred_element_type=F32)
        sums[pl.ds(b * TILE, TILE), :] = SHARE * total


def spread_kernel(edge_ids, off, sums, far, roots, second, hop, offered, offered_on, edge_s, sem):
    row_count = second.shape[0]
    parity = lax.rem(lax.axis_index("group"), 2)
    copy = pltpu.make_async_copy(edge_ids, edge_s, sem)
    copy.start()
    chunk = row_count // SPREAD_CHUNKS
    for n in range(SPREAD_CHUNKS):
        rows = pl.ds(n * chunk, chunk)
        total = sums[rows, :] + jnp.dot(far[rows, :], off[...], preferred_element_type=F32)
        for k in range(chunk // TILE):
            b = n * (chunk // TILE) + k
            root = roots[:, b : b + 1]
            one = root * total[k * TILE : (k + 1) * TILE]
            hop[pl.ds(b * TILE, TILE), :] = one.astype(BF)
            second[pl.ds(b * TILE, TILE), :] = (root * one).astype(BF)
    copy.wait()
    for s in range(CAPG):
        block = pl.ds(pl.multiple_of(edge_s[0, parity, s] * TILE, TILE), TILE)
        offered[pl.ds(s * TILE, TILE), :] = second[block, :]
        block = pl.ds(pl.multiple_of(edge_s[0, 1 - parity, s] * TILE, TILE), TILE)
        offered_on[pl.ds(s * TILE, TILE), :] = second[block, :]


def rest_kernel(send_ids, second, hop, hot, wide, request, *rest):
    owners = send_ids.shape[1]
    inner_in = rest[: owners - 1]
    own, picked, *peers = rest[owners - 1 : -2]
    send_s, sem = rest[-2:]
    count = hot.shape[0]
    row_count, width = second.shape
    blocks = row_count // TILE
    mine = lax.axis_index("inner")
    copy = pltpu.make_async_copy(send_ids, send_s, sem)
    copy.start()
    total = jnp.dot(wide[...], second[...], preferred_element_type=F32)
    own[...] = request_scale(request, count, width) * total
    picked[...] = (TPB * jnp.dot(hot[...], hop[...], preferred_element_type=F32)).astype(BF)
    copy.wait()
    for k in range(1, owners):
        peer = lax.rem(mine - k + owners, owners)
        message = inner_in[k - 1]
        base = blocks + mine * CAP
        asked = jnp.concatenate(expanded(message, count, width, [base + s for s in range(CAP)]), axis=1)
        offered = [
            second[pl.ds(pl.multiple_of(send_s[0, peer, s] * TILE, TILE), TILE), :] for s in range(CAP)
        ]
        total = jnp.dot(asked, jnp.concatenate(offered, axis=0), preferred_element_type=F32)
        peers[k - 1][...] = (request_scale(message, count, width) * total).astype(BF)


def answer_kernel(group_base, off, offered, on, offered_on, to_off, to_on):
    count, width = to_off.shape
    parity = lax.rem(lax.axis_index("group"), 2)
    for request, rows, base, answer in (
        (off, offered, group_base + (1 - parity) * CAPG, to_off),
        (on, offered_on, group_base + parity * CAPG, to_on),
    ):
        asked = jnp.concatenate(expanded(request, count, width, [base + s for s in range(CAPG)]), axis=1)
        total = jnp.dot(asked, rows[...], preferred_element_type=F32)
        answer[...] = (request_scale(request, count, width) * total).astype(BF)


def merge_kernel(owners, off, on, own, picked, *rest):
    peers = rest[: owners - 1]
    bundles = rest[owners - 1 :]
    slots = bundles[0].shape[1]
    mine = lax.axis_index("inner")
    for k in range(owners):
        rows = pl.ds(pl.multiple_of(lax.rem(mine + k, owners) * slots, slots), slots)
        total = own[rows, :] + off[rows, :].astype(F32) + on[rows, :].astype(F32)
        bundles[k][0] = total.astype(BF)
        bundles[k][1] = picked[rows, :]
        for r in range(1, owners):
            bundles[k][1 + r] = peers[r - 1][rows, :]


def gather_kernel(owners, *refs):
    bundles, out = refs[:owners], refs[owners]
    slots, width = bundles[0].shape[1:]
    mine = lax.axis_index("inner")
    for p in range(owners):
        total = bundles[p][0].astype(F32)
        for k in range(owners):
            if k != p:
                total = total + bundles[k][1 + (p - k) % owners].astype(F32)
        part = lax.rem(mine - p + owners, owners)
        rows = pl.ds(pl.multiple_of(part * slots, slots), slots)
        out[rows, 0:width] = bundles[p][1]
        out[rows, width : 2 * width] = total.astype(BF)


VMEM = pl.BlockSpec(memory_space=pltpu.VMEM)
HBM = pl.BlockSpec(memory_space=pltpu.HBM)
ANY = pl.BlockSpec(memory_space=pl.ANY)


def call(kernel, name, inputs, specs, outputs, scratch=()):
    return pl.pallas_call(
        kernel,
        out_shape=outputs,
        in_specs=specs,
        out_specs=[VMEM] * len(outputs),
        scratch_shapes=list(scratch),
        compiler_params=pltpu.CompilerParams(vmem_limit_bytes=30 * 1024 * 1024),
        name=name,
    )(*inputs)


def on_device(groups, owners, features, projection, adjacency, degree, tile_src, send_ids, edge_ids, train_ids):
    row_count, depth = features.shape
    blocks = row_count // TILE
    width = projection.shape[1]
    slots = train_ids.shape[2]
    count = owners * slots
    tail = TPB * TILE // width * count + META
    degree = degree.reshape(blocks, TILE)
    tile_src = tile_src.T
    across = [(g, (g + (1 if g % 2 else -1)) % groups) for g in range(groups)]
    beside = [(g, g ^ 1) for g in range(groups)]

    def around(value, k):
        return lax.ppermute(value, "inner", [(i, (i + k) % owners) for i in range(owners)])

    def array(*shape, kind=BF):
        return jax.ShapeDtypeStruct(shape, kind)

    def smem(like):
        return pltpu.SMEM(like.shape, jnp.int32)

    degree_scratch = pltpu.VMEM((16, TILE), jnp.int32)
    dma = pltpu.SemaphoreType.DMA

    head = jnp.dot(features[: blocks * 7 // 12 * TILE], projection, preferred_element_type=F32)
    first, off, *outgoing = call(
        first_kernel,
        "first",
        (edge_ids, send_ids, degree, projection, features, head),
        [HBM] * 2 + [VMEM] * 4,
        [array(blocks, TILE, width), array(CAPG * TILE, width)]
        + [array(CAPG // ON_PARTS * TILE, width)] * ON_PARTS
        + [array(CAP * TILE, width)] * (owners - 1),
        [smem(edge_ids), smem(send_ids), degree_scratch, dma((2,))],
    )
    on, inner_out = outgoing[:ON_PARTS], outgoing[ON_PARTS:]
    off_in = lax.ppermute(off, "group", across)
    inner_in = [around(inner_out[k - 1], k) for k in range(1, owners)]
    on_in = [lax.ppermute(part, "group", beside) for part in on]
    (request,) = call(
        ask_kernel,
        "ask",
        (tile_src, train_ids, degree, first, adjacency),
        [HBM] + [VMEM] * 2 + [ANY, VMEM],
        [array(tail, width)],
        [smem(tile_src), degree_scratch, dma],
    )
    asked_off = lax.ppermute(request, "group", across)
    far, hot, roots, wide, ask = call(
        far_kernel,
        "far",
        (tile_src, train_ids, degree, adjacency, request),
        [HBM] + [VMEM] * 4,
        [
            array(row_count, CAPG * TILE),
            array(count, row_count),
            array(TILE, 16, kind=F32),
            array(count, row_count),
            array(tail, width),
        ],
        [smem(tile_src), degree_scratch, dma],
    )
    sums, ask = call(
        near_kernel,
        "near",
        (tile_src, first, adjacency, ask, *on_in, *inner_in),
        [HBM] * 2 + [VMEM] * (1 + ON_PARTS + owners),
        [array(row_count, width, kind=F32), array(tail, width)],
        [smem(tile_src), pltpu.VMEM((blocks + owners * CAP + 2 * CAPG, TILE, width), BF), dma((2,))],
    )
    asked_on = lax.ppermute(ask, "group", beside)
    asked_inner = [around(ask, k) for k in range(1, owners)]
    second, hop, offered, offered_on = call(
        spread_kernel,
        "spread",
        (edge_ids, off_in, sums, far, roots),
        [HBM] + [VMEM] * 4,
        [array(row_count, width)] * 2 + [array(CAPG * TILE, width)] * 2,
        [smem(edge_ids), dma],
    )
    to_off, to_on = call(
        functools.partial(answer_kernel, blocks + owners * CAP),
        "answer",
        (asked_off, offered, asked_on, offered_on),
        [VMEM] * 4,
        [array(count, width)] * 2,
    )
    own, picked, *peers = call(
        rest_kernel,
        "rest",
        (send_ids, second, hop, hot, wide, request, *asked_inner),
        [HBM] + [VMEM] * (4 + owners),
        [array(count, width, kind=F32)] + [array(count, width)] * owners,
        [smem(send_ids), dma],
    )
    off_part = lax.ppermute(to_off, "group", across)
    on_part = lax.ppermute(to_on, "group", beside)
    bundles = call(
        functools.partial(merge_kernel, owners),
        "merge",
        (off_part, on_part, own, picked, *peers),
        [VMEM] * (3 + owners),
        [array(1 + owners, slots, width)] * owners,
    )
    bundles = [bundles[0]] + [around(bundles[k], k) for k in range(1, owners)]
    return call(
        functools.partial(gather_kernel, owners), "gather", bundles, [VMEM] * owners, [array(count, 2 * width)]
    )[0]


def solution(mesh):
    both = ("group", "inner")

    def run(
        features, projection, adjacency, degree, tile_src, send_ids, send_count, edge_ids, edge_count, train_ids
    ):
        return on_device(
            mesh.shape["group"], mesh.shape["inner"],
            features, projection, adjacency, degree, tile_src, send_ids, edge_ids, train_ids,
        )

    placed = (
        P(both, None),
        P(),
        P(both, None),
        P(both),
        P(both, None),
        P(both, None, None),
        P(both, None),
        P(both, None, None),
        P(both, None),
        P(both, None, None),
    )
    return jax.shard_map(run, mesh=mesh, in_specs=placed, out_specs=P(both, None), check_vma=False)
```
